32 devices in a mesh: wide: 16 (over z, y, x), narrow: 2 (over core).
Axes of the slice: x: 2, y: 2, z: 4, core: 2. Of those that a mesh axis runs over, the one named last changes fastest.
Arguments:
- loads: bfloat16 [16, 2, 64, 1024], P('wide', 'narrow'), may hold values from -30 to 30
- flexibility: bfloat16 [16, 2, 1024, 1024], P('wide', 'narrow'), may hold values from -1 to 6
- dirichlet: bfloat16 [16, 2, 1024, 1024], P('wide', 'narrow'), may hold values from -1 to 6
- modes: bfloat16 [16, 2, 32, 1024], P('wide', 'narrow'), may hold values from -0.75 to 0.75
- coarse_inverse: bfloat16 [512, 512], P('wide', 'narrow'), may hold values from -1 to 4
- mode_counts: int32 [2, 16], replicated, may hold values from 1 to 32, 256 in all within a row
Outputs:
- multipliers: bfloat16 [16, 2, 64, 1024], P('wide', 'narrow')
- residual: bfloat16 [16, 2, 64, 1024], P('wide', 'narrow')
The draws below stay inside these ranges and needn't reach their ends.
Inputs may be any that keep to these rules, and one draw needn't show every extreme that they name: `mode_counts`: each row of this array is one grid column; the counts of each grid column sum to exactly 256 in all, and the largest count of each grid column is exactly 32.
All inputs are finite; a program needn't handle non-finite values.
Results may differ from the reference program's by a relative error of at most 0.0087.
The reference program's roundings to bfloat16 on the way (of `disp`, `rounded`, `inner`, `smoothed`, `weights`, `coarse_values` and `picked`) count: a program that leaves them out, or rounds other values in their place, can miss the bound.
Values may be sent and summed in bfloat16 or wider, within the bound.
A program may use at most 64 MiB of HBM per device.

```python
import math
import jax
import jax.numpy as jnp
import numpy as np
from jax import lax

B = 1024
LOADS = 64
MAXM = 32
ITERS = 2
ROWS = 16
COLS = 2
MCOL = 256
NC = 512


def spd_stack(key, diag_low, diag_high, off_scale):

    def one_block(block_index):
        sub_key = jax.random.fold_in(key, block_index)
        first_key, second_key = jax.random.split(sub_key)
        raw_noise = jax.random.normal(first_key, (B, B), jnp.float32)
        symmetric = (raw_noise + raw_noise.T) * (off_scale / math.sqrt(2.0 * B))
        diagonal = jax.random.uniform(second_key, (B,), jnp.float32, diag_low, diag_high)
        return (symmetric + jnp.diag(diagonal)).astype(jnp.bfloat16)
    blocks = lax.map(one_block, jnp.arange(ROWS * COLS))
    return blocks.reshape(ROWS, COLS, B, B)


def draw_flexibility(key, part):
    sub_key = jax.random.fold_in(key, 11)
    return spd_stack(sub_key, 1.5, 3.0, 0.6)


def draw_dirichlet(key, part):
    sub_key = jax.random.fold_in(key, 23)
    return spd_stack(sub_key, 1.5, 3.0, 0.6)


def draw_coarse_inverse(key, part):
    first_key, second_key = jax.random.split(jax.random.fold_in(key, 37))
    raw_noise = jax.random.normal(first_key, (NC, NC), jnp.float32)
    off_scale, low_end, high_end, partner_value = (0.4, 1.0, 2.0, 0.7)
    symmetric = (raw_noise + raw_noise.T) * (off_scale / math.sqrt(2.0 * NC))
    diagonal = jax.random.uniform(second_key, (NC,), jnp.float32, low_end, high_end)
    index_list = jnp.arange(NC, dtype=jnp.int32)
    partner_mask = jnp.logical_and(index_list[:, None] % MCOL == index_list[None, :] % MCOL, index_list[:, None] != index_list[None, :])
    partner_part = jnp.where(partner_mask, partner_value / (COLS - 1), 0.0).astype(jnp.float32)
    return (symmetric + partner_part + jnp.diag(diagonal)).astype(jnp.bfloat16)


def draw_loads(key, part):
    noise_key, scale_key = jax.random.split(jax.random.fold_in(key, 5))
    raw_noise = jnp.clip(jax.random.normal(noise_key, (ROWS, COLS, LOADS, B), jnp.float32), -4.0, 4.0)
    spread = jnp.exp(jax.random.uniform(scale_key, (ROWS, COLS, 1, 1), jnp.float32, 0.0, math.log(2.0)))
    ramp = 3.0 ** (jnp.arange(ROWS, dtype=jnp.float32) / max(ROWS - 1, 1))
    return (raw_noise * spread * ramp[:, None, None, None]).astype(jnp.bfloat16)


def block_levels(key, shape, cuts, least, top_value):
    loudness = 1.0
    for dim, shards_of in cuts:
        heights = jax.random.uniform(jax.random.fold_in(jax.random.fold_in(key, 6), dim), (shards_of,), jnp.float32, least / len(cuts), top_value / len(cuts))
        loudness = loudness * jnp.repeat(jnp.exp(heights), shape[dim] // shards_of).reshape((-1,) + (1,) * (len(shape) - 1 - dim))
    return loudness


def length_profile(number_of, total, most, lean):
    portions = [(1 << 20) // math.isqrt(grade ** lean) + 1 for grade in range(2, number_of + 1)]
    surplus, counts = total - most - (number_of - 1), [1] * (number_of - 1)
    while surplus > 0:
        candidates = [i for i in range(number_of - 1) if counts[i] < most]
        mass, remaining = sum([portions[i] for i in candidates]), surplus
        for i in candidates:
            extra = min(most - counts[i], max(1, remaining * portions[i] // mass), surplus)
            counts[i] = counts[i] + extra
            surplus = surplus - extra
    return np.array([most] + counts)


def ragged_sizes(own_key, amount, total, reach, lean):
    if amount == 2:
        one = jax.random.randint(own_key, (), max(1, total - reach), min(reach, total - 1) + 1)
        return jnp.stack([one, total - one])
    sizes = jnp.asarray(length_profile(amount, total, reach, lean), jnp.int32)
    couples = (amount - 1) // 2
    source_of, taker = sizes[1:1 + 2 * couples:2], sizes[2:2 + 2 * couples:2]
    margin = jnp.minimum(source_of - 1, reach - taker)
    passed = jax.random.randint(jax.random.fold_in(own_key, 1), (couples,), 0, 1 << 20) % (margin + 1)
    sizes = sizes.at[1:1 + 2 * couples:2].set(source_of - passed).at[2:2 + 2 * couples:2].set(taker + passed)
    return sizes[jax.random.permutation(jax.random.fold_in(own_key, 2), amount)]


def bell_draw(own_key, extent, scale, reach, shards=(), kind=jnp.bfloat16):
    loudness = block_levels(own_key, extent, shards, -0.22, 0.18) if shards else 1.0
    entries = jax.random.normal(own_key, extent, jnp.float32) * scale * loudness
    return jnp.minimum(jnp.maximum(entries, -reach), reach).astype(kind)


def setup_inputs(seed: int = 0) -> dict:
    splits = jax.random.split(jax.random.key(seed), 7)
    loads = draw_loads(jax.random.fold_in(splits[6], 71), 0)
    flexibility = draw_flexibility(jax.random.fold_in(splits[6], 71), 0)
    dirichlet = draw_dirichlet(jax.random.fold_in(splits[6], 71), 0)
    modes = bell_draw(splits[3], (ROWS, COLS, MAXM, B), 0.125, 0.75, ((0, 16), (1, 2)))
    coarse_inverse = draw_coarse_inverse(jax.random.fold_in(splits[6], 71), 0)
    mode_counts = jax.vmap(lambda own: ragged_sizes(own, ROWS, MCOL, MAXM, 2))(jax.random.split(splits[5], COLS)).reshape((COLS, ROWS)).astype(jnp.int32)
    return {"loads": loads, "flexibility": flexibility, "dirichlet": dirichlet, "modes": modes, "coarse_inverse": coarse_inverse, "mode_counts": mode_counts}


def jump_all(values):
    row_count, col_count, load_count, width = values.shape
    face_len = width // 4
    face_parts = values.astype(jnp.float32).reshape(row_count, col_count, load_count, 4, face_len)
    north_face = face_parts[:, :, :, 0]
    south_face = face_parts[:, :, :, 1]
    west_face = face_parts[:, :, :, 2]
    east_face = face_parts[:, :, :, 3]
    zero_row = jnp.zeros_like(north_face[:1])
    zero_col = jnp.zeros_like(north_face[:, :1])
    from_above = jnp.concatenate([zero_row, south_face[:-1]], axis=0)
    from_below = jnp.concatenate([north_face[1:], zero_row], axis=0)
    from_west = jnp.concatenate([zero_col, east_face[:, :-1]], axis=1)
    from_east = jnp.concatenate([west_face[:, 1:], zero_col], axis=1)
    nearby = jnp.stack([from_above, from_below, from_west, from_east], axis=3)
    return (face_parts - nearby).reshape(values.shape)


def block_products(values, blocks):
    def one_product(operands):
        return jnp.dot(operands[0], operands[1], preferred_element_type=jnp.float32)
    flat_values = values.reshape((-1,) + values.shape[2:])
    flat_blocks = blocks.reshape((-1,) + blocks.shape[2:])
    result = lax.map(one_product, (flat_values, flat_blocks))
    return result.reshape(values.shape[:2] + result.shape[1:])


def coarse_tables(mode_counts):
    end_points = jnp.cumsum(mode_counts, axis=1).astype(jnp.int32)
    starts = (end_points - mode_counts).astype(jnp.int32)
    position = jnp.arange(MCOL, dtype=jnp.int32)
    owner_row = jnp.sum((end_points[:, None, :] <= position[None, :, None]).astype(jnp.int32), axis=2)
    slot_index = owner_row * MAXM + position[None, :] - jnp.take_along_axis(starts, owner_row, axis=1)
    return starts, slot_index


def coarse_part(rounded, modes, coarse_inverse, mode_counts, starts, slot_index):
    row_count, col_count, load_count = rounded.shape[0], rounded.shape[1], rounded.shape[2]
    weights = block_products(rounded, jnp.swapaxes(modes, 2, 3)).astype(jnp.bfloat16)
    pieces = []
    for column in range(col_count):
        padded = jnp.transpose(weights[:, column], (1, 0, 2)).reshape(load_count, row_count * MAXM)
        pieces.append(jnp.take(padded, slot_index[column], axis=0 + 1))
    gathered = jnp.concatenate(pieces, axis=1)
    coarse_values = jnp.dot(gathered, coarse_inverse.T, preferred_element_type=jnp.float32).astype(jnp.bfloat16)
    rank_list = jnp.arange(MAXM, dtype=jnp.int32)
    column_base = (jnp.arange(col_count, dtype=jnp.int32) * MCOL)[:, None, None]
    own_index = jnp.minimum(column_base + starts[:, :, None] + rank_list, NC - 1).astype(jnp.int32)
    is_valid = rank_list < mode_counts[:, :, None]
    picked = jnp.take(coarse_values, own_index.reshape(-1), axis=1).reshape(load_count, col_count, row_count, MAXM)
    picked = jnp.where(is_valid[None], picked, jnp.zeros_like(picked))
    picked = jnp.transpose(picked, (2, 1, 0, 3))
    return block_products(picked, modes)


def reference(loads, flexibility, dirichlet, modes, coarse_inverse, mode_counts):
    starts, slot_index = coarse_tables(mode_counts)

    def precondition(values):
        rounded = values.astype(jnp.bfloat16)
        inner = jump_all(rounded).astype(jnp.bfloat16)
        smoothed = block_products(inner, dirichlet).astype(jnp.bfloat16)
        return jump_all(smoothed) + coarse_part(rounded, modes, coarse_inverse, mode_counts, starts, slot_index)

    def load_dot(left, right):
        return jnp.sum(left * right, axis=(0, 1, 3))

    disp = block_products(loads, flexibility).astype(jnp.bfloat16)
    residual = jump_all(disp)
    multipliers = jnp.zeros_like(residual)
    direction = precondition(residual)
    energy = load_dot(residual, direction)
    for step_number in range(ITERS):
        moved = jump_all(direction.astype(jnp.bfloat16)).astype(jnp.bfloat16)
        image = jump_all(block_products(moved, flexibility).astype(jnp.bfloat16))
        step_size = energy / load_dot(direction, image)
        multipliers = multipliers + step_size[:, None] * direction
        residual = residual - step_size[:, None] * image
        if step_number + 1 < ITERS:
            fresh_z = precondition(residual)
            fresh = load_dot(residual, fresh_z)
            direction = fresh_z + (fresh / energy)[:, None] * direction
            energy = fresh
    return multipliers.astype(jnp.bfloat16), residual.astype(jnp.bfloat16)
```

```python
import functools

import jax
import jax.numpy as jnp
from jax import lax
from jax.experimental import pallas as pl
from jax.experimental.pallas import tpu as pltpu
from jax.sharding import PartitionSpec as P

MESH = pl.DeviceIdType.MESH
ITERS = 2
FACES = 4
OPPOSITE = (1, 0, 3, 2)
F32 = jnp.float32
BF16 = jnp.bfloat16


def mm(left, right):
    return jnp.dot(left, right, preferred_element_type=F32)


def mm_nt(left, right):
    return lax.dot_general(left, right, (((1,), (1,)), ((), ())), preferred_element_type=F32)


def mm_tn(left, right):
    return mm(left.T.astype(BF16), right)


def kernel(
    rows, cols, loads_hbm, flex_hbm, dirichlet_hbm, modes_hbm, inverse_hbm, counts_ref,
    mult_ref, resid_ref,
    loads, flex, dirichlet, modes, inverse, near_modes, weight_table, pick_table,
    weight_box, value_box, sum_box, out_face, in_face, moved, r_f, d_f, g_f, z_f, gz_f, x_f,
    load_sem, face_send, face_recv, setup_send, setup_recv, bulk_send, bulk_recv,
):
    total = rows * cols
    i = lax.axis_index("wide")
    j = lax.axis_index("narrow")
    me = i * cols + j
    cases = loads.shape[0]
    face = loads.shape[1] // FACES
    slots = modes.shape[0]
    half = slots // 2
    block_rows, column_width = inverse.shape[1], inverse.shape[2]
    block_half = block_rows // 2
    order = cols * column_width

    exists = (i > 0, i < rows - 1, j > 0, j < cols - 1)
    across = ((i - 1, j), (i + 1, j), (i, j - 1), (i, j + 1))
    have = [jnp.where(e, 1.0, 0.0).astype(F32) for e in exists]
    scale = [1.0 + h for h in have]

    def device(k):
        target = lax.rem(me + k, total)
        return (target // cols, lax.rem(target, cols))

    barrier = pltpu.get_barrier_semaphore()

    @pl.loop(1, total)
    def _(k):
        pl.semaphore_signal(barrier, inc=1, device_id=device(k), device_id_type=MESH)

    def fetch(source, target, number):
        copy = pltpu.make_async_copy(source, target, load_sem.at[number])
        copy.start()
        return copy

    get_loads = fetch(loads_hbm, loads, 0)
    get_flex = [
        fetch(flex_hbm.at[:, pl.ds(f * face, face)], flex.at[f], 1 + f) for f in range(FACES)
    ]
    get_modes = fetch(modes_hbm, modes, 9)
    get_inverse = fetch(inverse_hbm, inverse.at[j], 10)
    get_dirichlet = [
        fetch(dirichlet_hbm.at[:, pl.ds(f * face, face)], dirichlet.at[f], 5 + f)
        for f in range(FACES)
    ]

    for f in range(FACES):
        @pl.when(jnp.logical_not(exists[f]))
        def _():
            in_face[:, f] = jnp.zeros((in_face.shape[0], cases, face), BF16)
            near_modes[f] = jnp.zeros((slots, face), BF16)

    def face_copy(use, f):
        return pltpu.make_async_remote_copy(
            src_ref=out_face.at[use, f],
            dst_ref=in_face.at[use, OPPOSITE[f]],
            send_sem=face_send.at[use, f],
            recv_sem=face_recv.at[use, OPPOSITE[f]],
            device_id=across[f],
            device_id_type=MESH,
        )

    def face_start(use, f):
        @pl.when(exists[f])
        def _():
            face_copy(use, f).start()

    def face_wait(use, f):
        @pl.when(exists[f])
        def _():
            pltpu.make_async_remote_copy(
                src_ref=out_face.at[use, f],
                dst_ref=in_face.at[use, f],
                send_sem=face_send.at[use, f],
                recv_sem=face_recv.at[use, f],
                device_id=across[f],
                device_id_type=MESH,
            ).wait_recv()

    def modes_copy(f, slot):
        return pltpu.make_async_remote_copy(
            src_ref=modes.at[:, pl.ds(f * face, face)],
            dst_ref=near_modes.at[slot],
            send_sem=setup_send.at[f],
            recv_sem=setup_recv.at[slot],
            device_id=across[f],
            device_id_type=MESH,
        )

    def bulk(box, number, slot, target):
        return pltpu.make_async_remote_copy(
            src_ref=box.at[slot],
            dst_ref=box.at[slot],
            send_sem=bulk_send.at[number],
            recv_sem=bulk_recv.at[number],
            device_id=target,
            device_id_type=MESH,
        )

    def to_all(box, number):
        @pl.loop(1, total)
        def _(k):
            bulk(box, number, me, device(k)).start()

    def to_column(box, number):
        @pl.loop(1, rows)
        def _(k):
            bulk(box, number, i, (lax.rem(i + k, rows), j)).start()

    def to_row(box, number):
        @pl.loop(1, cols)
        def _(k):
            bulk(box, number, j, (i, lax.rem(j + k, cols))).start()

    def all_of(box, number):
        most = box.shape[0] - 1
        return pltpu.make_async_remote_copy(
            src_ref=box.at[pl.ds(0, most)],
            dst_ref=box.at[pl.ds(0, most)],
            send_sem=bulk_send.at[number],
            recv_sem=bulk_recv.at[number],
            device_id=device(1),
            device_id_type=MESH,
        )

    def row_sum(field):
        part = field[:, : face // 2] + field[:, face // 2 :]
        while part.shape[1] > 128:
            part = part[:, : part.shape[1] // 2] + part[:, part.shape[1] // 2 :]
        part = jnp.concatenate([part, jnp.zeros((128 - cases, 128), F32)], axis=0)
        return jnp.sum(part.T, axis=0, keepdims=True)

    def as_column(row):
        part = jnp.broadcast_to(row, (128, 128)).T[:cases]
        return jnp.concatenate([part] * (face // 128), axis=1)

    def share_sum(number, row):
        box = sum_box.at[number]
        box[pl.ds(me, 1)] = row[None]
        to_all(box, number)

    def take_sum(number):
        box = sum_box.at[number]
        all_of(box, number).wait_recv()
        return jnp.sum(box[...], axis=0)

    sums = 2 * ITERS

    def pack(values):
        low = values.shape[0] // 2
        return jnp.concatenate([values[:low], values[low:]], axis=1)

    get_loads.wait()
    for f in range(FACES):
        get_flex[f].wait()
        out_face[0, f] = mm(loads[...], flex[f]).astype(BF16)
        if f == 0:
            pl.semaphore_wait(barrier, total - 1)
        face_start(0, f)

    get_modes.wait()
    get_inverse.wait()
    for f in range(FACES):
        @pl.when(exists[f])
        def _():
            modes_copy(f, OPPOSITE[f]).start()
    to_row(inverse, sums)

    counts = counts_ref[...].astype(F32).astype(BF16)
    tile = min(total * half, 512)
    chunk = min(column_width, 256)
    all_of(inverse, sums).wait_recv()

    @pl.loop(0, total * half // tile)
    def _(tile_index):
        at = pl.multiple_of(tile_index * tile, tile)
        lane = at + lax.broadcasted_iota(jnp.int32, (rows, tile), 1)
        row_of = lane // (half * cols)
        down = lax.broadcasted_iota(jnp.int32, (rows, tile), 0)
        begin = mm(counts, jnp.where(down < row_of, 1.0, 0.0).astype(BF16))
        count = mm(counts, jnp.where(down == row_of, 1.0, 0.0).astype(BF16))
        lane_c = at + lax.broadcasted_iota(jnp.int32, (cols, tile), 1)
        column_of = lax.rem(lane_c // half, cols)
        which = lax.broadcasted_iota(jnp.int32, (cols, tile), 0)
        mine = which == column_of
        begin = begin + (column_of * column_width).astype(F32)
        begin = jnp.sum(jnp.where(mine, begin, 0.0), axis=0, keepdims=True)
        count = jnp.sum(jnp.where(mine, count, 0.0), axis=0, keepdims=True)
        lane_1 = at + lax.broadcasted_iota(jnp.int32, (1, tile), 1)
        rank = lax.rem(lane_1, half).astype(F32)
        for h in range(2):
            slot = rank + float(h * half)
            number = jnp.where(slot < count, begin + slot, -1.0)
            gathered = jnp.zeros((block_rows, tile), F32)
            for column in range(cols):
                def add(c, carry, column=column, number=number):
                    first = pl.multiple_of(c * chunk, chunk)
                    down_b = lax.broadcasted_iota(jnp.int32, (chunk, tile), 0)
                    b = (down_b + (column * column_width + first)).astype(F32)
                    hot = jnp.where(b == number, 1.0, 0.0).astype(BF16)
                    return carry + mm(inverse[column, :, pl.ds(first, chunk)], hot)
                gathered = lax.fori_loop(0, column_width // chunk, add, gathered)
            block_down = lax.broadcasted_iota(jnp.int32, (block_rows, tile), 0)
            own = (block_down + i * block_rows).astype(F32)
            weight_table[pl.ds(h * block_rows, block_rows), pl.ds(at, tile)] = gathered.astype(BF16)
            weight_table[pl.ds((2 + h) * block_rows, block_rows), pl.ds(at, tile)] = jnp.where(
                own == number, 1.0, 0.0
            ).astype(BF16)

    count_f = counts_ref[...].astype(F32)
    down = lax.broadcasted_iota(jnp.int32, (cols, rows), 0)
    along = lax.broadcasted_iota(jnp.int32, (cols, rows), 1)

    def pick(row, column):
        begin = jnp.sum(
            jnp.where((down == column) & (along < row), count_f, 0.0), keepdims=True
        )
        count = jnp.sum(
            jnp.where((down == column) & (along == row), count_f, 0.0), keepdims=True
        )
        return begin + (column * column_width).astype(F32), count

    for s, (row, column) in enumerate(((i, j),) + across):
        begin, count = pick(row, column)
        rank = lax.broadcasted_iota(jnp.int32, (slots, 1), 0).astype(F32)
        number = jnp.where(rank < count, begin + rank, -1.0)
        lane = lax.broadcasted_iota(jnp.int32, (slots, rows * block_half), 1)
        for h in range(2):
            a = (lane // block_half) * block_rows + lax.rem(lane, block_half) + h * block_half
            pick_table[h, pl.ds(s * slots, slots)] = jnp.where(
                a.astype(F32) == number, 1.0, 0.0
            ).astype(BF16)

    for f in range(FACES):
        face_wait(0, f)
        r_f[f] = out_face[0, f].astype(F32) - in_face[0, f].astype(F32)

    def precondition(turn, use):
        w_box, v_box = weight_box.at[turn], value_box.at[turn]
        w_number, v_number = sums + 1 + 2 * turn, sums + 2 + 2 * turn
        weights = jnp.zeros((slots, cases), F32)
        for f in range(FACES):
            rounded = r_f[f].astype(BF16)
            weights = weights + mm_nt(modes[:, f * face : (f + 1) * face], rounded)
            moved[:, f * face : (f + 1) * face] = (rounded.astype(F32) * scale[f]).astype(BF16)
        w_box[pl.ds(me, 1)] = pack(weights).astype(BF16)[None]
        to_all(w_box, w_number)

        total_f = jnp.zeros((cases, face), F32)
        for f in range(FACES):
            if turn == 0:
                get_dirichlet[f].wait()
            smoothed = mm(moved[...], dirichlet[f]).astype(BF16)
            out_face[use, f] = smoothed
            face_start(use, f)
            total_f = total_f + (r_f[f] * scale[f]) * smoothed.astype(F32)
        row = row_sum(total_f)

        all_of(w_box, w_number).wait_recv()
        out = mm(weight_table[...], w_box[...].reshape(total * half, 2 * cases))
        b = block_rows
        values = (out[:b, :cases] + out[b : 2 * b, cases:]).astype(BF16)
        own = out[2 * b : 3 * b, :cases] + out[3 * b :, cases:]
        v_box[pl.ds(i, 1)] = pack(values.astype(F32)).astype(BF16)[None]
        to_column(v_box, v_number)
        inner = jnp.sum(values.astype(F32) * own, axis=0, keepdims=True)
        inner = jnp.concatenate([inner, jnp.zeros((1, 128 - cases), F32)], axis=1)
        row = row + inner * jnp.where(j == 0, 1.0, 0.0)
        share_sum(2 * turn, row)

        for f in range(FACES):
            face_wait(use, f)
            local = out_face[use, f].astype(F32) - in_face[use, f].astype(F32)
            z_f[f] = local
            gz_f[f] = -local * have[f]
        if turn == 0:
            for f in range(FACES):
                @pl.when(exists[f])
                def _():
                    modes_copy(f, f).wait_recv()

        all_of(v_box, v_number).wait_recv()
        flat = v_box[...].reshape(rows * block_half, 2 * cases)
        picked = mm(pick_table[0], flat)[:, :cases] + mm(pick_table[1], flat)[:, cases:]
        own_picked = picked[:slots].T.astype(BF16)
        for f in range(FACES):
            z_f[f] = z_f[f] + mm(own_picked, modes[:, f * face : (f + 1) * face])
            gz_f[f] = gz_f[f] + mm_tn(picked[(1 + f) * slots : (2 + f) * slots], near_modes[f])

    precondition(0, 1)
    energy = None
    use = 2
    for turn in range(ITERS):
        if turn == 0:
            for f in range(FACES):
                d_f[f] = z_f[f]
                g_f[f] = gz_f[f]
        else:
            fresh = take_sum(2 * turn)
            beta = as_column(fresh / energy)
            energy = fresh
            for f in range(FACES):
                d_f[f] = z_f[f] + beta * d_f[f]
                g_f[f] = gz_f[f] + beta * g_f[f]
        for f in range(FACES):
            moved[:, f * face : (f + 1) * face] = (
                d_f[f].astype(BF16).astype(F32) - g_f[f].astype(BF16).astype(F32)
            ).astype(BF16)
        total_f = jnp.zeros((cases, face), F32)
        for f in range(FACES):
            image = mm(moved[...], flex[f]).astype(BF16)
            out_face[use, f] = image
            face_start(use, f)
            total_f = total_f + (d_f[f] - g_f[f]) * image.astype(F32)
        share_sum(2 * turn + 1, row_sum(total_f))
        if turn == 0:
            energy = take_sum(0)
        for f in range(FACES):
            face_wait(use, f)
        step = as_column(energy / take_sum(2 * turn + 1))
        for f in range(FACES):
            image = out_face[use, f].astype(F32) - in_face[use, f].astype(F32)
            residual = r_f[f] - step * image
            advance = step * d_f[f]
            if turn > 0:
                advance = x_f[f] + advance
            if turn + 1 < ITERS:
                r_f[f] = residual
                x_f[f] = advance
            else:
                mult_ref[:, f * face : (f + 1) * face] = advance.astype(BF16)
                resid_ref[:, f * face : (f + 1) * face] = residual.astype(BF16)
        use += 1
        if turn + 1 < ITERS:
            precondition(turn + 1, use)
            use += 1

    for f in range(FACES):
        @pl.when(exists[f])
        def _():
            modes_copy(f, OPPOSITE[f]).wait_send()
            for use in range(2 * ITERS + 1):
                face_copy(use, f).wait_send()
    for number in range(sums):
        all_of(sum_box.at[number], number).wait_send()
    all_of(inverse, sums).wait_send()
    for turn in range(ITERS):
        all_of(weight_box.at[turn], sums + 1 + 2 * turn).wait_send()
        all_of(value_box.at[turn], sums + 2 + 2 * turn).wait_send()


def shards(rows, cols, loads, flexibility, dirichlet, modes, coarse_inverse, mode_counts):
    _, _, cases, width = loads.shape
    slots = modes.shape[2]
    block_rows, column_width = coarse_inverse.shape
    total = rows * cols
    face = width // FACES
    uses = 2 * ITERS + 1
    bulks = 2 * ITERS + 1 + 2 * ITERS
    anywhere = pl.BlockSpec(memory_space=pl.ANY)
    inside = pl.BlockSpec(memory_space=pltpu.VMEM)
    field = pltpu.VMEM((FACES, cases, face), F32)
    dma = pltpu.SemaphoreType.DMA
    mult, resid = pl.pallas_call(
        functools.partial(kernel, rows, cols),
        out_shape=[jax.ShapeDtypeStruct((cases, width), BF16)] * 2,
        in_specs=[anywhere] * 5 + [inside],
        out_specs=[inside] * 2,
        scratch_shapes=[
            pltpu.VMEM((cases, width), BF16),
            pltpu.VMEM((FACES, width, face), BF16),
            pltpu.VMEM((FACES, width, face), BF16),
            pltpu.VMEM((slots, width), BF16),
            pltpu.VMEM((cols, block_rows, column_width), BF16),
            pltpu.VMEM((FACES, slots, face), BF16),
            pltpu.VMEM((4 * block_rows, total * slots // 2), BF16),
            pltpu.VMEM((2, (1 + FACES) * slots, rows * block_rows // 2), BF16),
            pltpu.VMEM((ITERS, total, slots // 2, 2 * cases), BF16),
            pltpu.VMEM((ITERS, rows, block_rows // 2, 2 * cases), BF16),
            pltpu.VMEM((2 * ITERS, total, 1, 128), F32),
            pltpu.VMEM((uses, FACES, cases, face), BF16),
            pltpu.VMEM((uses, FACES, cases, face), BF16),
            pltpu.VMEM((cases, width), BF16),
            field, field, field, field, field, field,
            dma((11,)),
            dma((uses, FACES)),
            dma((uses, FACES)),
            dma((FACES,)),
            dma((FACES,)),
            dma((bulks,)),
            dma((bulks,)),
        ],
        compiler_params=pltpu.CompilerParams(
            collective_id=0, has_side_effects=True, vmem_limit_bytes=40 * 1024 * 1024
        ),
    )(
        loads.reshape(cases, width),
        flexibility.reshape(width, width),
        dirichlet.reshape(width, width),
        modes.reshape(slots, width),
        coarse_inverse,
        mode_counts,
    )
    return mult[None, None], resid[None, None]


def solution(mesh):
    return jax.shard_map(
        functools.partial(shards, mesh.shape["wide"], mesh.shape["narrow"]),
        mesh=mesh,
        in_specs=(
            P("wide", "narrow", None, None),
            P("wide", "narrow", None, None),
            P("wide", "narrow", None, None),
            P("wide", "narrow", None, None),
            P("wide", "narrow"),
            P(),
        ),
        out_specs=(P("wide", "narrow", None, None), P("wide", "narrow", None, None)),
        check_vma=False,
    )
```

```python
import functools

import jax
import jax.numpy as jnp
from jax import lax
from jax.experimental import pallas as pl
from jax.experimental.pallas import tpu as pltpu
from jax.sharding import PartitionSpec as P

MESH = pl.DeviceIdType.MESH
LOGICAL = pl.DeviceIdType.LOGICAL
ITERS = 2
FACES = 4
OPPOSITE = (1, 0, 3, 2)
F32 = jnp.float32
BF16 = jnp.bfloat16


def mm(left, right):
    return jnp.dot(left, right, preferred_element_type=F32)


def mm_nt(left, right):
    return lax.dot_general(left, right, (((1,), (1,)), ((), ())), preferred_element_type=F32)


def mm_tn(left, right):
    return mm(left.T.astype(BF16), right)


def kernel(
    rows, cols, loads_hbm, flex_hbm, dirichlet_hbm, modes_hbm, inverse_hbm, counts_ref,
    mult_ref, resid_ref,
    loads, flex, dirichlet, modes, inverse, near_modes, weight_table, pick_table,
    weight_box, value_box, sum_box, out_face, in_face, moved, r_f, d_f, g_f, z_f, gz_f, x_f,
    load_sem, face_send, face_recv, setup_send, setup_recv, bulk_send, bulk_recv,
):
    total = rows * cols
    i = lax.axis_index("wide")
    j = lax.axis_index("narrow")
    me = i * cols + j
    cases = loads.shape[0]
    face = loads.shape[1] // FACES
    slots = modes.shape[0]
    half = slots // 2
    block_rows, column_width = inverse.shape[1], inverse.shape[2]
    block_half = block_rows // 2
    order = cols * column_width

    exists = (i > 0, i < rows - 1, j > 0, j < cols - 1)
    across = ((i - 1, j), (i + 1, j), (i, j - 1), (i, j + 1))
    have = [jnp.where(e, 1.0, 0.0).astype(F32) for e in exists]
    scale = [1.0 + h for h in have]

    def device(k):
        return lax.rem(me + k, total)

    def repeat(last, body):
        if last <= 64:
            for k in range(1, last):
                body(k)
        else:
            pl.loop(1, last)(body)

    barrier = pltpu.get_barrier_semaphore()

    def greet(k):
        pl.semaphore_signal(barrier, inc=1, device_id=device(k), device_id_type=LOGICAL)

    repeat(total, greet)

    def fetch(source, target, number):
        copy = pltpu.make_async_copy(source, target, load_sem.at[number])
        copy.start()
        return copy

    get_loads = fetch(loads_hbm, loads, 0)
    get_flex = [
        fetch(flex_hbm.at[:, pl.ds(f * face, face)], flex.at[f], 1 + f) for f in range(FACES)
    ]
    get_modes = fetch(modes_hbm, modes, 9)
    get_inverse = fetch(inverse_hbm, inverse.at[j], 10)
    get_dirichlet = [
        fetch(dirichlet_hbm.at[:, pl.ds(f * face, face)], dirichlet.at[f], 5 + f)
        for f in range(FACES)
    ]

    for f in range(FACES):
        @pl.when(jnp.logical_not(exists[f]))
        def _():
            in_face[:, f] = jnp.zeros((in_face.shape[0], cases, face), BF16)
            near_modes[f] = jnp.zeros((slots, face), BF16)

    def face_copy(use, f):
        return pltpu.make_async_remote_copy(
            src_ref=out_face.at[use, f],
            dst_ref=in_face.at[use, OPPOSITE[f]],
            send_sem=face_send.at[use, f],
            recv_sem=face_recv.at[use, OPPOSITE[f]],
            device_id=across[f],
            device_id_type=MESH,
        )

    def face_start(use, f):
        @pl.when(exists[f])
        def _():
            face_copy(use, f).start()

    def face_wait(use, f):
        @pl.when(exists[f])
        def _():
            pltpu.make_async_remote_copy(
                src_ref=out_face.at[use, f],
                dst_ref=in_face.at[use, f],
                send_sem=face_send.at[use, f],
                recv_sem=face_recv.at[use, f],
                device_id=across[f],
                device_id_type=MESH,
            ).wait_recv()

    def modes_copy(f, slot):
        return pltpu.make_async_remote_copy(
            src_ref=modes.at[:, pl.ds(f * face, face)],
            dst_ref=near_modes.at[slot],
            send_sem=setup_send.at[f],
            recv_sem=setup_recv.at[slot],
            device_id=across[f],
            device_id_type=MESH,
        )

    def bulk(box, number, slot, target):
        return pltpu.make_async_remote_copy(
            src_ref=box.at[slot],
            dst_ref=box.at[slot],
            send_sem=bulk_send.at[number],
            recv_sem=bulk_recv.at[number],
            device_id=target,
            device_id_type=LOGICAL,
        )

    def to_all(box, number):
        repeat(total, lambda k: bulk(box, number, me, device(k)).start())

    def to_column(box, number):
        repeat(rows, lambda k: bulk(box, number, i, device(k * cols)).start())

    def to_row(box, number):
        repeat(cols, lambda k: bulk(box, number, j, i * cols + lax.rem(j + k, cols)).start())

    def all_of(box, number):
        most = box.shape[0] - 1
        return pltpu.make_async_remote_copy(
            src_ref=box.at[pl.ds(0, most)],
            dst_ref=box.at[pl.ds(0, most)],
            send_sem=bulk_send.at[number],
            recv_sem=bulk_recv.at[number],
            device_id=device(1),
            device_id_type=LOGICAL,
        )

    def row_sum(field):
        part = field[:, : face // 2] + field[:, face // 2 :]
        while part.shape[1] > 128:
            part = part[:, : part.shape[1] // 2] + part[:, part.shape[1] // 2 :]
        part = jnp.concatenate([part, jnp.zeros((128 - cases, 128), F32)], axis=0)
        return jnp.sum(part.T, axis=0, keepdims=True)

    def as_column(row):
        part = jnp.broadcast_to(row, (128, 128)).T[:cases]
        return jnp.concatenate([part] * (face // 128), axis=1)

    def share_sum(number, row):
        box = sum_box.at[number]
        box[pl.ds(me, 1)] = row[None]
        to_all(box, number)

    def take_sum(number):
        box = sum_box.at[number]
        all_of(box, number).wait_recv()
        return jnp.sum(box[...], axis=0)

    sums = 2 * ITERS

    def pack(values):
        low = values.shape[0] // 2
        return jnp.concatenate([values[:low], values[low:]], axis=1)

    get_loads.wait()
    for f in range(FACES):
        get_flex[f].wait()
        out_face[0, f] = mm(loads[...], flex[f]).astype(BF16)
        if f == 0:
            pl.semaphore_wait(barrier, total - 1)
        face_start(0, f)

    get_modes.wait()
    get_inverse.wait()
    for f in range(FACES):
        @pl.when(exists[f])
        def _():
            modes_copy(f, OPPOSITE[f]).start()
    to_row(inverse, sums)

    counts = counts_ref[...].astype(F32).astype(BF16)
    tile = min(total * half, 512)
    chunk = min(column_width, 256)
    all_of(inverse, sums).wait_recv()

    @pl.loop(0, total * half // tile)
    def _(tile_index):
        at = pl.multiple_of(tile_index * tile, tile)
        lane = at + lax.broadcasted_iota(jnp.int32, (rows, tile), 1)
        row_of = lane // (half * cols)
        down = lax.broadcasted_iota(jnp.int32, (rows, tile), 0)
        begin = mm(counts, jnp.where(down < row_of, 1.0, 0.0).astype(BF16))
        count = mm(counts, jnp.where(down == row_of, 1.0, 0.0).astype(BF16))
        lane_c = at + lax.broadcasted_iota(jnp.int32, (cols, tile), 1)
        column_of = lax.rem(lane_c // half, cols)
        which = lax.broadcasted_iota(jnp.int32, (cols, tile), 0)
        mine = which == column_of
        begin = begin + (column_of * column_width).astype(F32)
        begin = jnp.sum(jnp.where(mine, begin, 0.0), axis=0, keepdims=True)
        count = jnp.sum(jnp.where(mine, count, 0.0), axis=0, keepdims=True)
        lane_1 = at + lax.broadcasted_iota(jnp.int32, (1, tile), 1)
        rank = lax.rem(lane_1, half).astype(F32)
        for h in range(2):
            slot = rank + float(h * half)
            number = jnp.where(slot < count, begin + slot, -1.0)
            gathered = jnp.zeros((block_rows, tile), F32)
            for column in range(cols):
                def add(c, carry, column=column, number=number):
                    first = pl.multiple_of(c * chunk, chunk)
                    down_b = lax.broadcasted_iota(jnp.int32, (chunk, tile), 0)
                    b = (down_b + (column * column_width + first)).astype(F32)
                    hot = jnp.where(b == number, 1.0, 0.0).astype(BF16)
                    return carry + mm(inverse[column, :, pl.ds(first, chunk)], hot)
                gathered = lax.fori_loop(0, column_width // chunk, add, gathered)
            block_down = lax.broadcasted_iota(jnp.int32, (block_rows, tile), 0)
            own = (block_down + i * block_rows).astype(F32)
            weight_table[pl.ds(h * block_rows, block_rows), pl.ds(at, tile)] = gathered.astype(BF16)
            weight_table[pl.ds((2 + h) * block_rows, block_rows), pl.ds(at, tile)] = jnp.where(
                own == number, 1.0, 0.0
            ).astype(BF16)

    count_f = counts_ref[...].astype(F32)
    down = lax.broadcasted_iota(jnp.int32, (cols, rows), 0)
    along = lax.broadcasted_iota(jnp.int32, (cols, rows), 1)

    def pick(row, column):
        begin = jnp.sum(
            jnp.where((down == column) & (along < row), count_f, 0.0), keepdims=True
        )
        count = jnp.sum(
            jnp.where((down == column) & (along == row), count_f, 0.0), keepdims=True
        )
        return begin + (column * column_width).astype(F32), count

    for s, (row, column) in enumerate(((i, j),) + across):
        begin, count = pick(row, column)
        rank = lax.broadcasted_iota(jnp.int32, (slots, 1), 0).astype(F32)
        number = jnp.where(rank < count, begin + rank, -1.0)
        lane = lax.broadcasted_iota(jnp.int32, (slots, rows * block_half), 1)
        for h in range(2):
            a = (lane // block_half) * block_rows + lax.rem(lane, block_half) + h * block_half
            pick_table[h, pl.ds(s * slots, slots)] = jnp.where(
                a.astype(F32) == number, 1.0, 0.0
            ).astype(BF16)

    for f in range(FACES):
        face_wait(0, f)
        r_f[f] = out_face[0, f].astype(F32) - in_face[0, f].astype(F32)

    def precondition(turn, use):
        w_box, v_box = weight_box.at[turn], value_box.at[turn]
        w_number, v_number = sums + 1 + 2 * turn, sums + 2 + 2 * turn
        weights = jnp.zeros((slots, cases), F32)
        for f in range(FACES):
            rounded = r_f[f].astype(BF16)
            weights = weights + mm_nt(modes[:, f * face : (f + 1) * face], rounded)
            moved[:, f * face : (f + 1) * face] = (rounded.astype(F32) * scale[f]).astype(BF16)
        w_box[pl.ds(me, 1)] = pack(weights).astype(BF16)[None]
        to_all(w_box, w_number)

        total_f = jnp.zeros((cases, face), F32)
        for f in range(FACES):
            if turn == 0:
                get_dirichlet[f].wait()
            smoothed = mm(moved[...], dirichlet[f]).astype(BF16)
            out_face[use, f] = smoothed
            face_start(use, f)
            total_f = total_f + (r_f[f] * scale[f]) * smoothed.astype(F32)
        row = row_sum(total_f)

        all_of(w_box, w_number).wait_recv()
        out = mm(weight_table[...], w_box[...].reshape(total * half, 2 * cases))
        b = block_rows
        values = (out[:b, :cases] + out[b : 2 * b, cases:]).astype(BF16)
        own = out[2 * b : 3 * b, :cases] + out[3 * b :, cases:]
        v_box[pl.ds(i, 1)] = pack(values.astype(F32)).astype(BF16)[None]
        to_column(v_box, v_number)
        inner = jnp.sum(values.astype(F32) * own, axis=0, keepdims=True)
        inner = jnp.concatenate([inner, jnp.zeros((1, 128 - cases), F32)], axis=1)
        row = row + inner * jnp.where(j == 0, 1.0, 0.0)
        if turn > 0:
            share_sum(2 * turn, jnp.concatenate([row, row], axis=1))

        for f in range(FACES):
            face_wait(use, f)
            local = out_face[use, f].astype(F32) - in_face[use, f].astype(F32)
            z_f[f] = local
            gz_f[f] = -local * have[f]
        if turn == 0:
            for f in range(FACES):
                @pl.when(exists[f])
                def _():
                    modes_copy(f, f).wait_recv()

        all_of(v_box, v_number).wait_recv()
        flat = v_box[...].reshape(rows * block_half, 2 * cases)
        picked = mm(pick_table[0], flat)[:, :cases] + mm(pick_table[1], flat)[:, cases:]
        own_picked = picked[:slots].T.astype(BF16)
        for f in range(FACES):
            z_f[f] = z_f[f] + mm(own_picked, modes[:, f * face : (f + 1) * face])
            gz_f[f] = gz_f[f] + mm_tn(picked[(1 + f) * slots : (2 + f) * slots], near_modes[f])
        return row

    first_energy = precondition(0, 1)
    energy = None
    use = 2
    for turn in range(ITERS):
        if turn == 0:
            for f in range(FACES):
                d_f[f] = z_f[f]
                g_f[f] = gz_f[f]
        else:
            fresh = take_sum(2 * turn)[:, :128]
            beta = as_column(fresh / energy)
            energy = fresh
            for f in range(FACES):
                d_f[f] = z_f[f] + beta * d_f[f]
                g_f[f] = gz_f[f] + beta * g_f[f]
        for f in range(FACES):
            moved[:, f * face : (f + 1) * face] = (
                d_f[f].astype(BF16).astype(F32) - g_f[f].astype(BF16).astype(F32)
            ).astype(BF16)
        total_f = jnp.zeros((cases, face), F32)
        for f in range(FACES):
            image = mm(moved[...], flex[f]).astype(BF16)
            out_face[use, f] = image
            face_start(use, f)
            total_f = total_f + (d_f[f] - g_f[f]) * image.astype(F32)
        row = row_sum(total_f)
        share_sum(2 * turn + 1, jnp.concatenate([row, first_energy], axis=1))
        for f in range(FACES):
            face_wait(use, f)
        both = take_sum(2 * turn + 1)
        if turn == 0:
            energy = both[:, 128:]
        step = as_column(energy / both[:, :128])
        for f in range(FACES):
            image = out_face[use, f].astype(F32) - in_face[use, f].astype(F32)
            residual = r_f[f] - step * image
            advance = step * d_f[f]
            if turn > 0:
                advance = x_f[f] + advance
            if turn + 1 < ITERS:
                r_f[f] = residual
                x_f[f] = advance
            else:
                mult_ref[:, f * face : (f + 1) * face] = advance.astype(BF16)
                resid_ref[:, f * face : (f + 1) * face] = residual.astype(BF16)
        use += 1
        if turn + 1 < ITERS:
            precondition(turn + 1, use)
            use += 1

    for f in range(FACES):
        @pl.when(exists[f])
        def _():
            modes_copy(f, OPPOSITE[f]).wait_send()
            for use in range(2 * ITERS + 1):
                face_copy(use, f).wait_send()
    for number in range(1, sums):
        all_of(sum_box.at[number], number).wait_send()
    all_of(inverse, sums).wait_send()
    for turn in range(ITERS):
        all_of(weight_box.at[turn], sums + 1 + 2 * turn).wait_send()
        all_of(value_box.at[turn], sums + 2 + 2 * turn).wait_send()


def shards(rows, cols, loads, flexibility, dirichlet, modes, coarse_inverse, mode_counts):
    _, _, cases, width = loads.shape
    slots = modes.shape[2]
    block_rows, column_width = coarse_inverse.shape
    total = rows * cols
    face = width // FACES
    uses = 2 * ITERS + 1
    bulks = 2 * ITERS + 1 + 2 * ITERS
    anywhere = pl.BlockSpec(memory_space=pl.ANY)
    inside = pl.BlockSpec(memory_space=pltpu.VMEM)
    field = pltpu.VMEM((FACES, cases, face), F32)
    dma = pltpu.SemaphoreType.DMA
    mult, resid = pl.pallas_call(
        functools.partial(kernel, rows, cols),
        out_shape=[jax.ShapeDtypeStruct((cases, width), BF16)] * 2,
        in_specs=[anywhere] * 5 + [inside],
        out_specs=[inside] * 2,
        scratch_shapes=[
            pltpu.VMEM((cases, width), BF16),
            pltpu.VMEM((FACES, width, face), BF16),
            pltpu.VMEM((FACES, width, face), BF16),
            pltpu.VMEM((slots, width), BF16),
            pltpu.VMEM((cols, block_rows, column_width), BF16),
            pltpu.VMEM((FACES, slots, face), BF16),
            pltpu.VMEM((4 * block_rows, total * slots // 2), BF16),
            pltpu.VMEM((2, (1 + FACES) * slots, rows * block_rows // 2), BF16),
            pltpu.VMEM((ITERS, total, slots // 2, 2 * cases), BF16),
            pltpu.VMEM((ITERS, rows, block_rows // 2, 2 * cases), BF16),
            pltpu.VMEM((2 * ITERS, total, 1, 256), F32),
            pltpu.VMEM((uses, FACES, cases, face), BF16),
            pltpu.VMEM((uses, FACES, cases, face), BF16),
            pltpu.VMEM((cases, width), BF16),
            field, field, field, field, field, field,
            dma((11,)),
            dma((uses, FACES)),
            dma((uses, FACES)),
            dma((FACES,)),
            dma((FACES,)),
            dma((bulks,)),
            dma((bulks,)),
        ],
        compiler_params=pltpu.CompilerParams(
            collective_id=0, has_side_effects=True, vmem_limit_bytes=62 * 1024 * 1024
        ),
    )(
        loads.reshape(cases, width),
        flexibility.reshape(width, width),
        dirichlet.reshape(width, width),
        modes.reshape(slots, width),
        coarse_inverse,
        mode_counts,
    )
    return mult[None, None], resid[None, None]


def solution(mesh):
    return jax.shard_map(
        functools.partial(shards, mesh.shape["wide"], mesh.shape["narrow"]),
        mesh=mesh,
        in_specs=(
            P("wide", "narrow", None, None),
            P("wide", "narrow", None, None),
            P("wide", "narrow", None, None),
            P("wide", "narrow", None, None),
            P("wide", "narrow"),
            P(),
        ),
        out_specs=(P("wide", "narrow", None, None), P("wide", "narrow", None, None)),
        check_vma=False,
    )
```

```python
import functools

import jax
import jax.numpy as jnp
from jax import lax
from jax.experimental import pallas as pl
from jax.experimental.pallas import tpu as pltpu
from jax.sharding import PartitionSpec as P

MESH = pl.DeviceIdType.MESH
LOGICAL = pl.DeviceIdType.LOGICAL
ITERS = 2
FACES = 4
OPPOSITE = (1, 0, 3, 2)
F32 = jnp.float32
BF16 = jnp.bfloat16


def mm(left, right):
    return jnp.dot(left, right, preferred_element_type=F32)


def mm_nt(left, right):
    return lax.dot_general(left, right, (((1,), (1,)), ((), ())), preferred_element_type=F32)


def mm_tn(left, right):
    return mm(left.T.astype(BF16), right)


def kernel(
    rows, cols, direct, loads_hbm, flex_hbm, dirichlet_hbm, modes_hbm, inverse_hbm, counts_hbm,
    mult_ref, resid_ref,
    loads, flex, dirichlet, modes, inverse, counts_ref, near_modes, weight_table, pick_table,
    weight_box, value_box, own_box, sum_box, out_face, in_face, moved, r_f, d_f, g_f, z_f, gz_f, x_f,
    load_sem, face_send, face_recv, setup_send, setup_recv, bulk_send, bulk_recv,
):
    total = rows * cols
    i = lax.axis_index("wide")
    j = lax.axis_index("narrow")
    me = i * cols + j
    cases = loads.shape[0]
    face = loads.shape[1] // FACES
    slots = modes.shape[0]
    half = slots // 2
    block_rows, column_width = inverse.shape[1], inverse.shape[2]
    block_half = block_rows // 2
    order = cols * column_width

    exists = (i > 0, i < rows - 1, j > 0, j < cols - 1)
    across = ((i - 1, j), (i + 1, j), (i, j - 1), (i, j + 1))
    have = [jnp.where(e, 1.0, 0.0).astype(F32) for e in exists]
    scale = [1.0 + h for h in have]

    def device(k):
        return lax.rem(me + k, total)

    def repeat(last, body):
        if last <= 64:
            for k in range(1, last):
                body(k)
        else:
            pl.loop(1, last)(body)

    barrier = pltpu.get_barrier_semaphore()

    def greet(k):
        pl.semaphore_signal(barrier, inc=1, device_id=device(k), device_id_type=LOGICAL)

    repeat(total, greet)

    def fetch(source, target, number):
        copy = pltpu.make_async_copy(source, target, load_sem.at[number])
        copy.start()
        return copy

    get_loads = fetch(loads_hbm, loads, 0)
    get_flex = [
        fetch(flex_hbm.at[:, pl.ds(f * face, face)], flex.at[f], 1 + f) for f in range(FACES)
    ]
    get_modes = fetch(modes_hbm, modes, 9)
    get_inverse = fetch(inverse_hbm, inverse.at[i if direct else j], 10)
    get_counts = fetch(counts_hbm, counts_ref, 11)
    get_dirichlet = [
        fetch(dirichlet_hbm.at[:, pl.ds(f * face, face)], dirichlet.at[f], 5 + f)
        for f in range(FACES)
    ]

    for f in range(FACES):
        @pl.when(jnp.logical_not(exists[f]))
        def _():
            in_face[:, f] = jnp.zeros((in_face.shape[0], cases, face), BF16)
            near_modes[f] = jnp.zeros((slots, face), BF16)

    def face_copy(use, f):
        return pltpu.make_async_remote_copy(
            src_ref=out_face.at[use, f],
            dst_ref=in_face.at[use, OPPOSITE[f]],
            send_sem=face_send.at[use, f],
            recv_sem=face_recv.at[use, OPPOSITE[f]],
            device_id=across[f],
            device_id_type=MESH,
        )

    def face_start(use, f):
        @pl.when(exists[f])
        def _():
            face_copy(use, f).start()

    def face_wait(use, f):
        @pl.when(exists[f])
        def _():
            pltpu.make_async_remote_copy(
                src_ref=out_face.at[use, f],
                dst_ref=in_face.at[use, f],
                send_sem=face_send.at[use, f],
                recv_sem=face_recv.at[use, f],
                device_id=across[f],
                device_id_type=MESH,
            ).wait_recv()

    def modes_copy(f, slot):
        return pltpu.make_async_remote_copy(
            src_ref=modes.at[:, pl.ds(f * face, face)],
            dst_ref=near_modes.at[slot],
            send_sem=setup_send.at[f],
            recv_sem=setup_recv.at[slot],
            device_id=across[f],
            device_id_type=MESH,
        )

    def bulk(box, number, slot, target):
        return pltpu.make_async_remote_copy(
            src_ref=box.at[slot],
            dst_ref=box.at[slot],
            send_sem=bulk_send.at[number],
            recv_sem=bulk_recv.at[number],
            device_id=target,
            device_id_type=LOGICAL,
        )

    def to_all(box, number):
        repeat(total, lambda k: bulk(box, number, me, device(k)).start())

    def to_column(box, number):
        repeat(rows, lambda k: bulk(box, number, i, device(k * cols)).start())

    def to_row(box, number):
        repeat(cols, lambda k: bulk(box, number, j, i * cols + lax.rem(j + k, cols)).start())

    def all_of(box, number):
        most = box.shape[0] - 1
        return pltpu.make_async_remote_copy(
            src_ref=box.at[pl.ds(0, most)],
            dst_ref=box.at[pl.ds(0, most)],
            send_sem=bulk_send.at[number],
            recv_sem=bulk_recv.at[number],
            device_id=device(1),
            device_id_type=LOGICAL,
        )

    def row_sum(field):
        part = field[:, : face // 2] + field[:, face // 2 :]
        while part.shape[1] > 128:
            part = part[:, : part.shape[1] // 2] + part[:, part.shape[1] // 2 :]
        part = jnp.concatenate([part, jnp.zeros((128 - cases, 128), F32)], axis=0)
        return jnp.sum(part.T, axis=0, keepdims=True)

    def as_column(row):
        part = jnp.broadcast_to(row, (128, 128)).T[:cases]
        return jnp.concatenate([part] * (face // 128), axis=1)

    def share_sum(number, row):
        box = sum_box.at[number]
        box[pl.ds(me, 1)] = row[None]
        to_all(box, number)

    def take_sum(number):
        box = sum_box.at[number]
        all_of(box, number).wait_recv()
        return jnp.sum(box[...], axis=0)

    sums = 2 * ITERS

    def pack(values):
        low = values.shape[0] // 2
        return jnp.concatenate([values[:low], values[low:]], axis=1)

    def unpack(values):
        values = values.astype(F32)
        return jnp.concatenate([values[:, :cases], values[:, cases:]], axis=0)

    def widen(row):
        return jnp.concatenate([row, jnp.zeros((1, 128 - cases), F32)], axis=1)

    get_loads.wait()
    for f in range(FACES):
        get_flex[f].wait()
        out_face[0, f] = mm(loads[...], flex[f]).astype(BF16)
        if f == 0:
            pl.semaphore_wait(barrier, total - 1)
        face_start(0, f)

    get_modes.wait()
    get_inverse.wait()
    for f in range(FACES):
        @pl.when(exists[f])
        def _():
            modes_copy(f, OPPOSITE[f]).start()
    if direct:
        to_column(inverse, sums)
    else:
        to_row(inverse, sums)

    get_counts.wait()
    counts = counts_ref[...].astype(F32).astype(BF16)

    def direct_table():
        span = rows * half
        lane = lax.broadcasted_iota(jnp.int32, (rows, span), 1)
        down = lax.broadcasted_iota(jnp.int32, (rows, span), 0)
        row_of = lane // half
        begin = mm(counts, jnp.where(down < row_of, 1.0, 0.0).astype(BF16))
        count = mm(counts, jnp.where(down == row_of, 1.0, 0.0).astype(BF16))
        mine = lax.broadcasted_iota(jnp.int32, (cols, span), 0) == j
        begin = jnp.sum(jnp.where(mine, begin, 0.0), axis=0, keepdims=True)
        count = jnp.sum(jnp.where(mine, count, 0.0), axis=0, keepdims=True)
        rank = lax.rem(lax.broadcasted_iota(jnp.int32, (1, span), 1), half).astype(F32)
        b = lax.broadcasted_iota(jnp.int32, (column_width, span), 0).astype(F32)
        for h in range(2):
            slot = rank + float(h * half)
            number = jnp.where(slot < count, begin + slot, -1.0)
            weight_table[pl.ds(order, column_width), pl.ds(h * span, span)] = jnp.where(
                b == number, 1.0, 0.0
            ).astype(BF16)
        all_of(inverse, sums).wait_recv()
        hot = weight_table[pl.ds(order, column_width), :]
        weight_table[pl.ds(0, order), :] = mm(
            inverse[...].reshape(order, column_width), hot
        ).astype(BF16)

    def spread_table():
        all_of(inverse, sums).wait_recv()
        tile = min(total * half, 512)
        chunk = min(column_width, 256)

        @pl.loop(0, total * half // tile)
        def _(tile_index):
            at = pl.multiple_of(tile_index * tile, tile)
            lane = at + lax.broadcasted_iota(jnp.int32, (rows, tile), 1)
            row_of = lane // (half * cols)
            down = lax.broadcasted_iota(jnp.int32, (rows, tile), 0)
            begin = mm(counts, jnp.where(down < row_of, 1.0, 0.0).astype(BF16))
            count = mm(counts, jnp.where(down == row_of, 1.0, 0.0).astype(BF16))
            lane_c = at + lax.broadcasted_iota(jnp.int32, (cols, tile), 1)
            column_of = lax.rem(lane_c // half, cols)
            which = lax.broadcasted_iota(jnp.int32, (cols, tile), 0)
            mine = which == column_of
            begin = begin + (column_of * column_width).astype(F32)
            begin = jnp.sum(jnp.where(mine, begin, 0.0), axis=0, keepdims=True)
            count = jnp.sum(jnp.where(mine, count, 0.0), axis=0, keepdims=True)
            lane_1 = at + lax.broadcasted_iota(jnp.int32, (1, tile), 1)
            rank = lax.rem(lane_1, half).astype(F32)
            for h in range(2):
                slot = rank + float(h * half)
                number = jnp.where(slot < count, begin + slot, -1.0)
                gathered = jnp.zeros((block_rows, tile), F32)
                for column in range(cols):
                    def add(c, carry, column=column, number=number):
                        first = pl.multiple_of(c * chunk, chunk)
                        down_b = lax.broadcasted_iota(jnp.int32, (chunk, tile), 0)
                        b = (down_b + (column * column_width + first)).astype(F32)
                        hot = jnp.where(b == number, 1.0, 0.0).astype(BF16)
                        return carry + mm(inverse[column, :, pl.ds(first, chunk)], hot)
                    gathered = lax.fori_loop(0, column_width // chunk, add, gathered)
                block_down = lax.broadcasted_iota(jnp.int32, (block_rows, tile), 0)
                own = (block_down + i * block_rows).astype(F32)
                weight_table[pl.ds(h * block_rows, block_rows), pl.ds(at, tile)] = gathered.astype(BF16)
                weight_table[pl.ds((2 + h) * block_rows, block_rows), pl.ds(at, tile)] = jnp.where(
                    own == number, 1.0, 0.0
                ).astype(BF16)

    if not direct:
        spread_table()

    count_f = counts_ref[...].astype(F32)
    down = lax.broadcasted_iota(jnp.int32, (cols, rows), 0)
    along = lax.broadcasted_iota(jnp.int32, (cols, rows), 1)

    def pick(row, column):
        begin = jnp.sum(
            jnp.where((down == column) & (along < row), count_f, 0.0), keepdims=True
        )
        count = jnp.sum(
            jnp.where((down == column) & (along == row), count_f, 0.0), keepdims=True
        )
        return begin + (column * column_width).astype(F32), count

    for s, (row, column) in enumerate(((i, j),) + across):
        begin, count = pick(row, column)
        rank = lax.broadcasted_iota(jnp.int32, (slots, 1), 0).astype(F32)
        number = jnp.where(rank < count, begin + rank, -1.0)
        if direct:
            lane = lax.broadcasted_iota(jnp.int32, (slots, order), 1)
            pick_table[0, pl.ds(s * slots, slots)] = jnp.where(
                lane.astype(F32) == number, 1.0, 0.0
            ).astype(BF16)
            continue
        lane = lax.broadcasted_iota(jnp.int32, (slots, rows * block_half), 1)
        for h in range(2):
            a = (lane // block_half) * block_rows + lax.rem(lane, block_half) + h * block_half
            pick_table[h, pl.ds(s * slots, slots)] = jnp.where(
                a.astype(F32) == number, 1.0, 0.0
            ).astype(BF16)

    for f in range(FACES):
        face_wait(0, f)
        r_f[f] = out_face[0, f].astype(F32) - in_face[0, f].astype(F32)

    def precondition(turn, use):
        w_box, v_box = weight_box.at[turn], value_box.at[turn]
        w_number, v_number, o_number = (sums + 1 + 3 * turn + n for n in range(3))
        weights = jnp.zeros((slots, cases), F32)
        for f in range(FACES):
            rounded = r_f[f].astype(BF16)
            weights = weights + mm_nt(modes[:, f * face : (f + 1) * face], rounded)
            moved[:, f * face : (f + 1) * face] = (rounded.astype(F32) * scale[f]).astype(BF16)
        if direct:
            w_box[pl.ds(i, 1)] = pack(weights).astype(BF16)[None]
            to_column(w_box, w_number)
        else:
            w_box[pl.ds(me, 1)] = pack(weights).astype(BF16)[None]
            to_all(w_box, w_number)

        total_f = jnp.zeros((cases, face), F32)
        for f in range(FACES):
            if turn == 0:
                get_dirichlet[f].wait()
            smoothed = mm(moved[...], dirichlet[f]).astype(BF16)
            out_face[use, f] = smoothed
            face_start(use, f)
            total_f = total_f + (r_f[f] * scale[f]) * smoothed.astype(F32)
        row = row_sum(total_f)

        both = jnp.concatenate([row, row], axis=1)
        if direct:
            if turn > 0:
                share_sum(2 * turn, both)
            else:
                direct_table()
            all_of(w_box, w_number).wait_recv()
            out = mm(weight_table[...], unpack(w_box[...].reshape(rows * half, 2 * cases)).astype(BF16))
            v_box[pl.ds(j, 1)] = pack(out[:order])[None]
            own_box[turn, pl.ds(j, 1)] = pack(out[order:]).astype(BF16)[None]
            to_row(v_box, v_number)
            to_row(own_box.at[turn], o_number)
        else:
            all_of(w_box, w_number).wait_recv()
            out = mm(weight_table[...], w_box[...].reshape(total * half, 2 * cases))
            b = block_rows
            values = (out[:b, :cases] + out[b : 2 * b, cases:]).astype(BF16)
            own = out[2 * b : 3 * b, :cases] + out[3 * b :, cases:]
            v_box[pl.ds(i, 1)] = pack(values.astype(F32)).astype(BF16)[None]
            to_column(v_box, v_number)
            inner = jnp.sum(values.astype(F32) * own, axis=0, keepdims=True)
            row = row + widen(inner) * jnp.where(j == 0, 1.0, 0.0)
            if turn > 0:
                share_sum(2 * turn, jnp.concatenate([row, row], axis=1))

        for f in range(FACES):
            face_wait(use, f)
            local = out_face[use, f].astype(F32) - in_face[use, f].astype(F32)
            z_f[f] = local
            gz_f[f] = -local * have[f]
        if turn == 0:
            for f in range(FACES):
                @pl.when(exists[f])
                def _():
                    modes_copy(f, f).wait_recv()

        all_of(v_box, v_number).wait_recv()
        extra = jnp.zeros((1, 128), F32)
        if direct:
            all_of(own_box.at[turn], o_number).wait_recv()
            values = unpack(jnp.sum(v_box[...], axis=0)).astype(BF16)
            own = jnp.concatenate([unpack(own_box[turn, k]) for k in range(cols)], axis=0)
            extra = widen(jnp.sum(values.astype(F32) * own, axis=0, keepdims=True))
            picked = mm(pick_table[0], values)
        else:
            flat = v_box[...].reshape(rows * block_half, 2 * cases)
            picked = mm(pick_table[0], flat)[:, :cases] + mm(pick_table[1], flat)[:, cases:]
        own_picked = picked[:slots].T.astype(BF16)
        for f in range(FACES):
            z_f[f] = z_f[f] + mm(own_picked, modes[:, f * face : (f + 1) * face])
            gz_f[f] = gz_f[f] + mm_tn(picked[(1 + f) * slots : (2 + f) * slots], near_modes[f])
        return row, extra

    first_energy, extra = precondition(0, 1)
    energy = None
    use = 2
    for turn in range(ITERS):
        if turn == 0:
            for f in range(FACES):
                d_f[f] = z_f[f]
                g_f[f] = gz_f[f]
        else:
            fresh = take_sum(2 * turn)[:, :128] + extra
            beta = as_column(fresh / energy)
            energy = fresh
            for f in range(FACES):
                d_f[f] = z_f[f] + beta * d_f[f]
                g_f[f] = gz_f[f] + beta * g_f[f]
        for f in range(FACES):
            moved[:, f * face : (f + 1) * face] = (
                d_f[f].astype(BF16).astype(F32) - g_f[f].astype(BF16).astype(F32)
            ).astype(BF16)
        total_f = jnp.zeros((cases, face), F32)
        for f in range(FACES):
            image = mm(moved[...], flex[f]).astype(BF16)
            out_face[use, f] = image
            face_start(use, f)
            total_f = total_f + (d_f[f] - g_f[f]) * image.astype(F32)
        row = row_sum(total_f)
        share_sum(2 * turn + 1, jnp.concatenate([row, first_energy], axis=1))
        for f in range(FACES):
            face_wait(use, f)
        both = take_sum(2 * turn + 1)
        if turn == 0:
            energy = both[:, 128:] + extra
        step = as_column(energy / both[:, :128])
        for f in range(FACES):
            image = out_face[use, f].astype(F32) - in_face[use, f].astype(F32)
            residual = r_f[f] - step * image
            advance = step * d_f[f]
            if turn > 0:
                advance = x_f[f] + advance
            if turn + 1 < ITERS:
                r_f[f] = residual
                x_f[f] = advance
            else:
                mult_ref[:, f * face : (f + 1) * face] = advance.astype(BF16)
                resid_ref[:, f * face : (f + 1) * face] = residual.astype(BF16)
        use += 1
        if turn + 1 < ITERS:
            _, extra = precondition(turn + 1, use)
            use += 1

    for f in range(FACES):
        @pl.when(exists[f])
        def _():
            modes_copy(f, OPPOSITE[f]).wait_send()
            for use in range(2 * ITERS + 1):
                face_copy(use, f).wait_send()
    for number in range(1, sums):
        all_of(sum_box.at[number], number).wait_send()
    all_of(inverse, sums).wait_send()
    for turn in range(ITERS):
        all_of(weight_box.at[turn], sums + 1 + 3 * turn).wait_send()
        all_of(value_box.at[turn], sums + 2 + 3 * turn).wait_send()
        if direct:
            all_of(own_box.at[turn], sums + 3 + 3 * turn).wait_send()


def settle(mult_in, resid_in, mult_out, resid_out, sem):
    first = pltpu.make_async_copy(mult_in, mult_out, sem.at[0])
    second = pltpu.make_async_copy(resid_in, resid_out, sem.at[1])
    first.start()
    second.start()
    first.wait()
    second.wait()


def shards(rows, cols, loads, flexibility, dirichlet, modes, coarse_inverse, mode_counts):
    _, _, cases, width = loads.shape
    slots = modes.shape[2]
    block_rows, column_width = coarse_inverse.shape
    total = rows * cols
    face = width // FACES
    uses = 2 * ITERS + 1
    bulks = 2 * ITERS + 1 + 3 * ITERS
    half, order = slots // 2, cols * column_width
    direct = order * column_width <= 1 << 20
    if direct:
        coarse = [
            pltpu.VMEM((order + column_width, rows * slots), BF16),
            pltpu.VMEM((1, (1 + FACES) * slots, order), BF16),
            pltpu.VMEM((ITERS, rows, half, 2 * cases), BF16),
            pltpu.VMEM((ITERS, cols, order // 2, 2 * cases), F32),
        ]
    else:
        coarse = [
            pltpu.VMEM((4 * block_rows, total * half), BF16),
            pltpu.VMEM((2, (1 + FACES) * slots, rows * block_rows // 2), BF16),
            pltpu.VMEM((ITERS, total, half, 2 * cases), BF16),
            pltpu.VMEM((ITERS, rows, block_rows // 2, 2 * cases), BF16),
        ]
    anywhere = pl.BlockSpec(memory_space=pl.ANY)
    inside = pl.BlockSpec(memory_space=pltpu.VMEM)
    field = pltpu.VMEM((FACES, cases, face), F32)
    dma = pltpu.SemaphoreType.DMA
    mult, resid = pl.pallas_call(
        functools.partial(kernel, rows, cols, direct),
        out_shape=[jax.ShapeDtypeStruct((cases, width), BF16)] * 2,
        in_specs=[anywhere] * 6,
        out_specs=[inside] * 2,
        scratch_shapes=[
            pltpu.VMEM((cases, width), BF16),
            pltpu.VMEM((FACES, width, face), BF16),
            pltpu.VMEM((FACES, width, face), BF16),
            pltpu.VMEM((slots, width), BF16),
            pltpu.VMEM((rows if direct else cols, block_rows, column_width), BF16),
            pltpu.VMEM((cols, rows), jnp.int32),
            pltpu.VMEM((FACES, slots, face), BF16),
            *coarse,
            pltpu.VMEM((ITERS, cols, column_width // 2, 2 * cases), BF16),
            pltpu.VMEM((2 * ITERS, total, 1, 256), F32),
            pltpu.VMEM((uses, FACES, cases, face), BF16),
            pltpu.VMEM((uses, FACES, cases, face), BF16),
            pltpu.VMEM((cases, width), BF16),
            field, field, field, field, field, field,
            dma((12,)),
            dma((uses, FACES)),
            dma((uses, FACES)),
            dma((FACES,)),
            dma((FACES,)),
            dma((bulks,)),
            dma((bulks,)),
        ],
        compiler_params=pltpu.CompilerParams(
            collective_id=0, has_side_effects=True, vmem_limit_bytes=62 * 1024 * 1024
        ),
    )(
        loads.reshape(cases, width),
        flexibility.reshape(width, width),
        dirichlet.reshape(width, width),
        modes.reshape(slots, width),
        coarse_inverse,
        mode_counts,
    )
    mult, resid = pl.pallas_call(
        settle,
        out_shape=[jax.ShapeDtypeStruct((cases, width), BF16)] * 2,
        in_specs=[anywhere] * 2,
        out_specs=[anywhere] * 2,
        scratch_shapes=[dma((2,))],
    )(mult, resid)
    return mult[None, None], resid[None, None]


def solution(mesh):
    return jax.shard_map(
        functools.partial(shards, mesh.shape["wide"], mesh.shape["narrow"]),
        mesh=mesh,
        in_specs=(
            P("wide", "narrow", None, None),
            P("wide", "narrow", None, None),
            P("wide", "narrow", None, None),
            P("wide", "narrow", None, None),
            P("wide", "narrow"),
            P(),
        ),
        out_specs=(P("wide", "narrow", None, None), P("wide", "narrow", None, None)),
        check_vma=False,
    )
```

```python
import functools

import jax
import jax.numpy as jnp
from jax import lax
from jax.experimental import pallas as pl
from jax.experimental.pallas import tpu as pltpu
from jax.sharding import PartitionSpec as P

MESH = pl.DeviceIdType.MESH
LOGICAL = pl.DeviceIdType.LOGICAL
ITERS = 2
FACES = 4
OPPOSITE = (1, 0, 3, 2)
F32 = jnp.float32
BF16 = jnp.bfloat16


def mm(left, right):
    return jnp.dot(left, right, preferred_element_type=F32)


def mm_nt(left, right):
    return lax.dot_general(left, right, (((1,), (1,)), ((), ())), preferred_element_type=F32)


def mm_tn(left, right):
    return mm(left.T.astype(BF16), right)


def kernel(
    rows, cols, direct, loads_hbm, flex_hbm, dirichlet_hbm, modes_hbm, inverse_hbm, counts_hbm,
    mult_ref, resid_ref,
    loads, flex, dirichlet, modes, inverse, counts_ref, near_modes, weight_table, pick_table,
    weight_box, value_box, own_box, sum_box, out_face, in_face, moved, r_f, d_f, g_f, z_f, gz_f, x_f,
    load_sem, face_send, face_recv, setup_send, setup_recv, bulk_send, bulk_recv,
):
    total = rows * cols
    i = lax.axis_index("wide")
    j = lax.axis_index("narrow")
    me = i * cols + j
    cases = loads.shape[0]
    face = loads.shape[1] // FACES
    slots = modes.shape[0]
    half = slots // 2
    block_rows, column_width = inverse.shape[1], inverse.shape[2]
    block_half = block_rows // 2
    order = cols * column_width

    exists = (i > 0, i < rows - 1, j > 0, j < cols - 1)
    across = ((i - 1, j), (i + 1, j), (i, j - 1), (i, j + 1))
    have = [jnp.where(e, 1.0, 0.0).astype(F32) for e in exists]
    scale = [1.0 + h for h in have]

    def device(k):
        return lax.rem(me + k, total)

    def repeat(last, body):
        if last <= 64:
            for k in sorted(range(1, last), key=lambda k: abs(2 * k - last)):
                body(k)
        else:
            pl.loop(1, last)(body)

    def fetch(source, target, number):
        copy = pltpu.make_async_copy(source, target, load_sem.at[number])
        copy.start()
        return copy

    get_loads = fetch(loads_hbm, loads, 0)
    get_flex = [
        fetch(flex_hbm.at[:, pl.ds(f * face, face)], flex.at[f], 1 + f) for f in range(FACES)
    ]
    barrier = pltpu.get_barrier_semaphore()

    def greet(k):
        pl.semaphore_signal(barrier, inc=1, device_id=device(k), device_id_type=LOGICAL)

    repeat(total, greet)

    get_modes = fetch(modes_hbm, modes, 9)
    get_inverse = fetch(inverse_hbm, inverse.at[i if direct else j], 10)
    get_counts = fetch(counts_hbm, counts_ref, 11)
    get_dirichlet = [
        fetch(dirichlet_hbm.at[:, pl.ds(f * face, face)], dirichlet.at[f], 5 + f)
        for f in range(FACES)
    ]

    for f in range(FACES):
        @pl.when(jnp.logical_not(exists[f]))
        def _():
            in_face[:, f] = jnp.zeros((in_face.shape[0], cases, face), BF16)
            near_modes[f] = jnp.zeros((slots, face), BF16)

    def face_copy(use, f):
        return pltpu.make_async_remote_copy(
            src_ref=out_face.at[use, f],
            dst_ref=in_face.at[use, OPPOSITE[f]],
            send_sem=face_send.at[use, f],
            recv_sem=face_recv.at[use, OPPOSITE[f]],
            device_id=across[f],
            device_id_type=MESH,
        )

    def face_start(use, f):
        @pl.when(exists[f])
        def _():
            face_copy(use, f).start()

    def face_wait(use, f):
        @pl.when(exists[f])
        def _():
            pltpu.make_async_remote_copy(
                src_ref=out_face.at[use, f],
                dst_ref=in_face.at[use, f],
                send_sem=face_send.at[use, f],
                recv_sem=face_recv.at[use, f],
                device_id=across[f],
                device_id_type=MESH,
            ).wait_recv()

    def modes_copy(f, slot):
        return pltpu.make_async_remote_copy(
            src_ref=modes.at[:, pl.ds(f * face, face)],
            dst_ref=near_modes.at[slot],
            send_sem=setup_send.at[f],
            recv_sem=setup_recv.at[slot],
            device_id=across[f],
            device_id_type=MESH,
        )

    def bulk(box, number, slot, target):
        return pltpu.make_async_remote_copy(
            src_ref=box.at[slot],
            dst_ref=box.at[slot],
            send_sem=bulk_send.at[number],
            recv_sem=bulk_recv.at[number],
            device_id=target,
            device_id_type=LOGICAL,
        )

    def to_all(box, number):
        repeat(total, lambda k: bulk(box, number, me, device(k)).start())

    def to_column(box, number):
        repeat(rows, lambda k: bulk(box, number, i, device(k * cols)).start())

    def to_row(box, number):
        repeat(cols, lambda k: bulk(box, number, j, i * cols + lax.rem(j + k, cols)).start())

    def all_of(box, number):
        most = box.shape[0] - 1
        return pltpu.make_async_remote_copy(
            src_ref=box.at[pl.ds(0, most)],
            dst_ref=box.at[pl.ds(0, most)],
            send_sem=bulk_send.at[number],
            recv_sem=bulk_recv.at[number],
            device_id=device(1),
            device_id_type=LOGICAL,
        )

    def row_sum(field):
        part = field[:, : face // 2] + field[:, face // 2 :]
        while part.shape[1] > 128:
            part = part[:, : part.shape[1] // 2] + part[:, part.shape[1] // 2 :]
        part = jnp.concatenate([part, jnp.zeros((128 - cases, 128), F32)], axis=0)
        return jnp.sum(part.T, axis=0, keepdims=True)

    def as_column(row):
        part = jnp.broadcast_to(row, (128, 128)).T[:cases]
        return jnp.concatenate([part] * (face // 128), axis=1)

    def share_sum(number, row):
        box = sum_box.at[number]
        box[pl.ds(me, 1)] = row[None]
        to_all(box, number)

    def take_sum(number):
        box = sum_box.at[number]
        all_of(box, number).wait_recv()
        return jnp.sum(box[...], axis=0)

    sums = 2 * ITERS

    def pack(values):
        low = values.shape[0] // 2
        return jnp.concatenate([values[:low], values[low:]], axis=1)

    def unpack(values):
        values = values.astype(F32)
        return jnp.concatenate([values[:, :cases], values[:, cases:]], axis=0)

    def widen(row):
        return jnp.concatenate([row, jnp.zeros((1, 128 - cases), F32)], axis=1)

    get_loads.wait()
    for f in range(FACES):
        get_flex[f].wait()
        out_face[0, f] = mm(loads[...], flex[f]).astype(BF16)
        if f == 0:
            pl.semaphore_wait(barrier, total - 1)
        face_start(0, f)

    get_modes.wait()
    get_inverse.wait()
    for f in range(FACES):
        @pl.when(exists[f])
        def _():
            modes_copy(f, OPPOSITE[f]).start()
    if direct:
        to_column(inverse, sums)
    else:
        to_row(inverse, sums)

    get_counts.wait()
    counts = counts_ref[...].astype(F32).astype(BF16)

    def direct_table():
        span = rows * half
        lane = lax.broadcasted_iota(jnp.int32, (rows, span), 1)
        down = lax.broadcasted_iota(jnp.int32, (rows, span), 0)
        row_of = lane // half
        begin = mm(counts, jnp.where(down < row_of, 1.0, 0.0).astype(BF16))
        count = mm(counts, jnp.where(down == row_of, 1.0, 0.0).astype(BF16))
        mine = lax.broadcasted_iota(jnp.int32, (cols, span), 0) == j
        begin = jnp.sum(jnp.where(mine, begin, 0.0), axis=0, keepdims=True)
        count = jnp.sum(jnp.where(mine, count, 0.0), axis=0, keepdims=True)
        rank = lax.rem(lax.broadcasted_iota(jnp.int32, (1, span), 1), half).astype(F32)
        b = lax.broadcasted_iota(jnp.int32, (column_width, span), 0).astype(F32)
        for h in range(2):
            slot = rank + float(h * half)
            number = jnp.where(slot < count, begin + slot, -1.0)
            weight_table[pl.ds(order, column_width), pl.ds(h * span, span)] = jnp.where(
                b == number, 1.0, 0.0
            ).astype(BF16)
        all_of(inverse, sums).wait_recv()
        hot = weight_table[pl.ds(order, column_width), :]
        weight_table[pl.ds(0, order), :] = mm(
            inverse[...].reshape(order, column_width), hot
        ).astype(BF16)

    def spread_table():
        all_of(inverse, sums).wait_recv()
        tile = min(total * half, 512)
        chunk = min(column_width, 256)

        @pl.loop(0, total * half // tile)
        def _(tile_index):
            at = pl.multiple_of(tile_index * tile, tile)
            lane = at + lax.broadcasted_iota(jnp.int32, (rows, tile), 1)
            row_of = lane // (half * cols)
            down = lax.broadcasted_iota(jnp.int32, (rows, tile), 0)
            begin = mm(counts, jnp.where(down < row_of, 1.0, 0.0).astype(BF16))
            count = mm(counts, jnp.where(down == row_of, 1.0, 0.0).astype(BF16))
            lane_c = at + lax.broadcasted_iota(jnp.int32, (cols, tile), 1)
            column_of = lax.rem(lane_c // half, cols)
            which = lax.broadcasted_iota(jnp.int32, (cols, tile), 0)
            mine = which == column_of
            begin = begin + (column_of * column_width).astype(F32)
            begin = jnp.sum(jnp.where(mine, begin, 0.0), axis=0, keepdims=True)
            count = jnp.sum(jnp.where(mine, count, 0.0), axis=0, keepdims=True)
            lane_1 = at + lax.broadcasted_iota(jnp.int32, (1, tile), 1)
            rank = lax.rem(lane_1, half).astype(F32)
            for h in range(2):
                slot = rank + float(h * half)
                number = jnp.where(slot < count, begin + slot, -1.0)
                gathered = jnp.zeros((block_rows, tile), F32)
                for column in range(cols):
                    def add(c, carry, column=column, number=number):
                        first = pl.multiple_of(c * chunk, chunk)
                        down_b = lax.broadcasted_iota(jnp.int32, (chunk, tile), 0)
                        b = (down_b + (column * column_width + first)).astype(F32)
                        hot = jnp.where(b == number, 1.0, 0.0).astype(BF16)
                        return carry + mm(inverse[column, :, pl.ds(first, chunk)], hot)
                    gathered = lax.fori_loop(0, column_width // chunk, add, gathered)
                block_down = lax.broadcasted_iota(jnp.int32, (block_rows, tile), 0)
                own = (block_down + i * block_rows).astype(F32)
                weight_table[pl.ds(h * block_rows, block_rows), pl.ds(at, tile)] = gathered.astype(BF16)
                weight_table[pl.ds((2 + h) * block_rows, block_rows), pl.ds(at, tile)] = jnp.where(
                    own == number, 1.0, 0.0
                ).astype(BF16)

    if not direct:
        spread_table()

    count_f = counts_ref[...].astype(F32)
    down = lax.broadcasted_iota(jnp.int32, (cols, rows), 0)
    along = lax.broadcasted_iota(jnp.int32, (cols, rows), 1)

    def pick(row, column):
        begin = jnp.sum(
            jnp.where((down == column) & (along < row), count_f, 0.0), keepdims=True
        )
        count = jnp.sum(
            jnp.where((down == column) & (along == row), count_f, 0.0), keepdims=True
        )
        return begin + (column * column_width).astype(F32), count

    for s, (row, column) in enumerate(((i, j),) + across):
        begin, count = pick(row, column)
        rank = lax.broadcasted_iota(jnp.int32, (slots, 1), 0).astype(F32)
        number = jnp.where(rank < count, begin + rank, -1.0)
        if direct:
            lane = lax.broadcasted_iota(jnp.int32, (slots, order), 1)
            pick_table[0, pl.ds(s * slots, slots)] = jnp.where(
                lane.astype(F32) == number, 1.0, 0.0
            ).astype(BF16)
            continue
        lane = lax.broadcasted_iota(jnp.int32, (slots, rows * block_half), 1)
        for h in range(2):
            a = (lane // block_half) * block_rows + lax.rem(lane, block_half) + h * block_half
            pick_table[h, pl.ds(s * slots, slots)] = jnp.where(
                a.astype(F32) == number, 1.0, 0.0
            ).astype(BF16)

    for f in range(FACES):
        face_wait(0, f)
        r_f[f] = out_face[0, f].astype(F32) - in_face[0, f].astype(F32)

    def precondition(turn, use):
        w_box, v_box = weight_box.at[turn], value_box.at[turn]
        w_number, v_number, o_number = (sums + 1 + 3 * turn + n for n in range(3))
        weights = jnp.zeros((slots, cases), F32)
        for f in range(FACES):
            rounded = r_f[f].astype(BF16)
            weights = weights + mm_nt(modes[:, f * face : (f + 1) * face], rounded)
            moved[:, f * face : (f + 1) * face] = (rounded.astype(F32) * scale[f]).astype(BF16)
        if direct:
            w_box[pl.ds(i, 1)] = pack(weights).astype(BF16)[None]
            to_column(w_box, w_number)
        else:
            w_box[pl.ds(me, 1)] = pack(weights).astype(BF16)[None]
            to_all(w_box, w_number)

        total_f = jnp.zeros((cases, face), F32)
        for f in range(FACES):
            if turn == 0:
                get_dirichlet[f].wait()
            smoothed = mm(moved[...], dirichlet[f]).astype(BF16)
            out_face[use, f] = smoothed
            face_start(use, f)
            total_f = total_f + (r_f[f] * scale[f]) * smoothed.astype(F32)
        row = row_sum(total_f)

        both = jnp.concatenate([row, row], axis=1)
        if direct:
            if turn > 0:
                share_sum(2 * turn, both)
            else:
                direct_table()
            all_of(w_box, w_number).wait_recv()
            out = mm(weight_table[...], unpack(w_box[...].reshape(rows * half, 2 * cases)).astype(BF16))
            v_box[pl.ds(j, 1)] = pack(out[:order])[None]
            own_box[turn, pl.ds(j, 1)] = pack(out[order:]).astype(BF16)[None]
            to_row(v_box, v_number)
            to_row(own_box.at[turn], o_number)
        else:
            all_of(w_box, w_number).wait_recv()
            out = mm(weight_table[...], w_box[...].reshape(total * half, 2 * cases))
            b = block_rows
            values = (out[:b, :cases] + out[b : 2 * b, cases:]).astype(BF16)
            own = out[2 * b : 3 * b, :cases] + out[3 * b :, cases:]
            v_box[pl.ds(i, 1)] = pack(values.astype(F32)).astype(BF16)[None]
            to_column(v_box, v_number)
            inner = jnp.sum(values.astype(F32) * own, axis=0, keepdims=True)
            row = row + widen(inner) * jnp.where(j == 0, 1.0, 0.0)
            if turn > 0:
                share_sum(2 * turn, jnp.concatenate([row, row], axis=1))

        for f in range(FACES):
            face_wait(use, f)
            local = out_face[use, f].astype(F32) - in_face[use, f].astype(F32)
            z_f[f] = local
            gz_f[f] = -local * have[f]
        if turn == 0:
            for f in range(FACES):
                @pl.when(exists[f])
                def _():
                    modes_copy(f, f).wait_recv()

        all_of(v_box, v_number).wait_recv()
        extra = jnp.zeros((1, 128), F32)
        if direct:
            all_of(own_box.at[turn], o_number).wait_recv()
            values = unpack(jnp.sum(v_box[...], axis=0)).astype(BF16)
            own = jnp.concatenate([unpack(own_box[turn, k]) for k in range(cols)], axis=0)
            extra = widen(jnp.sum(values.astype(F32) * own, axis=0, keepdims=True))
            picked = mm(pick_table[0], values)
        else:
            flat = v_box[...].reshape(rows * block_half, 2 * cases)
            picked = mm(pick_table[0], flat)[:, :cases] + mm(pick_table[1], flat)[:, cases:]
        own_picked = picked[:slots].T.astype(BF16)
        for f in range(FACES):
            z_f[f] = z_f[f] + mm(own_picked, modes[:, f * face : (f + 1) * face])
            gz_f[f] = gz_f[f] + mm_tn(picked[(1 + f) * slots : (2 + f) * slots], near_modes[f])
        return row, extra

    first_energy, extra = precondition(0, 1)
    energy = None
    use = 2
    for turn in range(ITERS):
        if turn == 0:
            for f in range(FACES):
                d_f[f] = z_f[f]
                g_f[f] = gz_f[f]
        else:
            fresh = take_sum(2 * turn)[:, :128] + extra
            beta = as_column(fresh / energy)
            energy = fresh
            for f in range(FACES):
                d_f[f] = z_f[f] + beta * d_f[f]
                g_f[f] = gz_f[f] + beta * g_f[f]
        for f in range(FACES):
            moved[:, f * face : (f + 1) * face] = (
                d_f[f].astype(BF16).astype(F32) - g_f[f].astype(BF16).astype(F32)
            ).astype(BF16)
        total_f = jnp.zeros((cases, face), F32)
        for f in range(FACES):
            image = mm(moved[...], flex[f]).astype(BF16)
            out_face[use, f] = image
            face_start(use, f)
            total_f = total_f + (d_f[f] - g_f[f]) * image.astype(F32)
        row = row_sum(total_f)
        share_sum(2 * turn + 1, jnp.concatenate([row, first_energy], axis=1))
        for f in range(FACES):
            face_wait(use, f)
        both = take_sum(2 * turn + 1)
        if turn == 0:
            energy = both[:, 128:] + extra
        step = as_column(energy / both[:, :128])
        for f in range(FACES):
            image = out_face[use, f].astype(F32) - in_face[use, f].astype(F32)
            residual = r_f[f] - step * image
            advance = step * d_f[f]
            if turn > 0:
                advance = x_f[f] + advance
            if turn + 1 < ITERS:
                r_f[f] = residual
                x_f[f] = advance
            else:
                mult_ref[:, f * face : (f + 1) * face] = advance.astype(BF16)
                resid_ref[:, f * face : (f + 1) * face] = residual.astype(BF16)
        use += 1
        if turn + 1 < ITERS:
            _, extra = precondition(turn + 1, use)
            use += 1

    for f in range(FACES):
        @pl.when(exists[f])
        def _():
            modes_copy(f, OPPOSITE[f]).wait_send()
            for use in range(2 * ITERS + 1):
                face_copy(use, f).wait_send()
    for number in range(1, sums):
        all_of(sum_box.at[number], number).wait_send()
    all_of(inverse, sums).wait_send()
    for turn in range(ITERS):
        all_of(weight_box.at[turn], sums + 1 + 3 * turn).wait_send()
        all_of(value_box.at[turn], sums + 2 + 3 * turn).wait_send()
        if direct:
            all_of(own_box.at[turn], sums + 3 + 3 * turn).wait_send()


def settle(mult_in, resid_in, mult_out, resid_out):
    mult_out[...] = mult_in[...]
    resid_out[...] = resid_in[...]


def shards(rows, cols, loads, flexibility, dirichlet, modes, coarse_inverse, mode_counts):
    _, _, cases, width = loads.shape
    slots = modes.shape[2]
    block_rows, column_width = coarse_inverse.shape
    total = rows * cols
    face = width // FACES
    uses = 2 * ITERS + 1
    bulks = 2 * ITERS + 1 + 3 * ITERS
    half, order = slots // 2, cols * column_width
    direct = order * column_width <= 1 << 20
    if direct:
        coarse = [
            pltpu.VMEM((order + column_width, rows * slots), BF16),
            pltpu.VMEM((1, (1 + FACES) * slots, order), BF16),
            pltpu.VMEM((ITERS, rows, half, 2 * cases), BF16),
            pltpu.VMEM((ITERS, cols, order // 2, 2 * cases), F32),
        ]
    else:
        coarse = [
            pltpu.VMEM((4 * block_rows, total * half), BF16),
            pltpu.VMEM((2, (1 + FACES) * slots, rows * block_rows // 2), BF16),
            pltpu.VMEM((ITERS, total, half, 2 * cases), BF16),
            pltpu.VMEM((ITERS, rows, block_rows // 2, 2 * cases), BF16),
        ]
    anywhere = pl.BlockSpec(memory_space=pl.ANY)
    inside = pl.BlockSpec(memory_space=pltpu.VMEM)
    field = pltpu.VMEM((FACES, cases, face), F32)
    dma = pltpu.SemaphoreType.DMA
    mult, resid = pl.pallas_call(
        functools.partial(kernel, rows, cols, direct),
        out_shape=[jax.ShapeDtypeStruct((cases, width), BF16)] * 2,
        in_specs=[anywhere] * 6,
        out_specs=[inside] * 2,
        scratch_shapes=[
            pltpu.VMEM((cases, width), BF16),
            pltpu.VMEM((FACES, width, face), BF16),
            pltpu.VMEM((FACES, width, face), BF16),
            pltpu.VMEM((slots, width), BF16),
            pltpu.VMEM((rows if direct else cols, block_rows, column_width), BF16),
            pltpu.VMEM((cols, rows), jnp.int32),
            pltpu.VMEM((FACES, slots, face), BF16),
            *coarse,
            pltpu.VMEM((ITERS, cols, column_width // 2, 2 * cases), BF16),
            pltpu.VMEM((2 * ITERS, total, 1, 256), F32),
            pltpu.VMEM((uses, FACES, cases, face), BF16),
            pltpu.VMEM((uses, FACES, cases, face), BF16),
            pltpu.VMEM((cases, width), BF16),
            field, field, field, field, field, field,
            dma((12,)),
            dma((uses, FACES)),
            dma((uses, FACES)),
            dma((FACES,)),
            dma((FACES,)),
            dma((bulks,)),
            dma((bulks,)),
        ],
        compiler_params=pltpu.CompilerParams(
            collective_id=0, has_side_effects=True, vmem_limit_bytes=62 * 1024 * 1024
        ),
    )(
        loads.reshape(cases, width),
        flexibility.reshape(width, width),
        dirichlet.reshape(width, width),
        modes.reshape(slots, width),
        coarse_inverse,
        mode_counts,
    )
    mult, resid = pl.pallas_call(
        settle,
        out_shape=[jax.ShapeDtypeStruct((cases, width), BF16)] * 2,
        in_specs=[inside] * 2,
        out_specs=[inside] * 2,
        compiler_params=pltpu.CompilerParams(vmem_limit_bytes=62 * 1024 * 1024),
    )(mult, resid)
    return mult[None, None], resid[None, None]


def solution(mesh):
    return jax.shard_map(
        functools.partial(shards, mesh.shape["wide"], mesh.shape["narrow"]),
        mesh=mesh,
        in_specs=(
            P("wide", "narrow", None, None),
            P("wide", "narrow", None, None),
            P("wide", "narrow", None, None),
            P("wide", "narrow", None, None),
            P("wide", "narrow"),
            P(),
        ),
        out_specs=(P("wide", "narrow", None, None), P("wide", "narrow", None, None)),
        check_vma=False,
    )
```

```python
import functools

import jax
import jax.numpy as jnp
from jax import lax
from jax.experimental import pallas as pl
from jax.experimental.pallas import tpu as pltpu
from jax.sharding import PartitionSpec as P

MESH = pl.DeviceIdType.MESH
LOGICAL = pl.DeviceIdType.LOGICAL
ITERS = 2
FACES = 4
OPPOSITE = (1, 0, 3, 2)
PAIRS = ((0, 1), (2, 3))
F32 = jnp.float32
BF16 = jnp.bfloat16


def mm(left, right):
    return jnp.dot(left, right, preferred_element_type=F32)


def mm_nt(left, right):
    return lax.dot_general(left, right, (((1,), (1,)), ((), ())), preferred_element_type=F32)


def mm_tn(left, right):
    return mm(left.T.astype(BF16), right)


def kernel(
    rows, cols, direct, loads_hbm, flex_hbm, dirichlet_hbm, modes_hbm, inverse_hbm, counts_hbm,
    mult_ref, resid_ref,
    loads, flex, dirichlet, modes, inverse, counts_ref, near_modes, weight_table, pick_table,
    weight_box, value_box, own_box, sum_box, out_face, in_face, moved, r_f, d_f, g_f, z_f, gz_f, x_f,
    load_sem, face_send, face_recv, setup_send, setup_recv, bulk_send, bulk_recv,
):
    total = rows * cols
    i = lax.axis_index("wide")
    j = lax.axis_index("narrow")
    me = i * cols + j
    cases = loads.shape[0]
    face = loads.shape[1] // FACES
    slots = modes.shape[0]
    half = slots // 2
    block_rows, column_width = inverse.shape[1], inverse.shape[2]
    block_half = block_rows // 2
    order = cols * column_width

    exists = (i > 0, i < rows - 1, j > 0, j < cols - 1)
    across = ((i - 1, j), (i + 1, j), (i, j - 1), (i, j + 1))
    have = [jnp.where(e, 1.0, 0.0).astype(F32) for e in exists]
    scale = [1.0 + h for h in have]

    def device(k):
        return lax.rem(me + k, total)

    def repeat(last, body):
        if last <= 64:
            for k in sorted(range(1, last), key=lambda k: abs(2 * k - last)):
                body(k)
        else:
            pl.loop(1, last)(body)

    def fetch(source, target, number):
        copy = pltpu.make_async_copy(source, target, load_sem.at[number])
        copy.start()
        return copy

    get_loads = fetch(loads_hbm, loads, 0)
    get_flex = [
        fetch(flex_hbm.at[:, pl.ds(f * face, face)], flex.at[f], 1 + f) for f in range(FACES)
    ]
    barrier = pltpu.get_barrier_semaphore()

    def greet(k):
        pl.semaphore_signal(barrier, inc=1, device_id=device(k), device_id_type=LOGICAL)

    repeat(total, greet)

    get_modes = fetch(modes_hbm, modes, 9)
    get_inverse = fetch(inverse_hbm, inverse.at[i if direct else j], 10)
    get_counts = fetch(counts_hbm, counts_ref, 11)
    get_dirichlet = [
        fetch(dirichlet_hbm.at[:, pl.ds(f * face, face)], dirichlet.at[f], 5 + f)
        for f in range(FACES)
    ]

    for f in range(FACES):
        @pl.when(jnp.logical_not(exists[f]))
        def _():
            in_face[:, f] = jnp.zeros((in_face.shape[0], cases, face), BF16)
            near_modes[f] = jnp.zeros((slots, face), BF16)

    def face_copy(use, f):
        return pltpu.make_async_remote_copy(
            src_ref=out_face.at[use, f],
            dst_ref=in_face.at[use, OPPOSITE[f]],
            send_sem=face_send.at[use, f],
            recv_sem=face_recv.at[use, OPPOSITE[f]],
            device_id=across[f],
            device_id_type=MESH,
        )

    def face_start(use, f):
        @pl.when(exists[f])
        def _():
            face_copy(use, f).start()

    def face_wait(use, f):
        @pl.when(exists[f])
        def _():
            pltpu.make_async_remote_copy(
                src_ref=out_face.at[use, f],
                dst_ref=in_face.at[use, f],
                send_sem=face_send.at[use, f],
                recv_sem=face_recv.at[use, f],
                device_id=across[f],
                device_id_type=MESH,
            ).wait_recv()

    def modes_copy(f, slot):
        return pltpu.make_async_remote_copy(
            src_ref=modes.at[:, pl.ds(f * face, face)],
            dst_ref=near_modes.at[slot],
            send_sem=setup_send.at[f],
            recv_sem=setup_recv.at[slot],
            device_id=across[f],
            device_id_type=MESH,
        )

    def bulk(box, number, slot, target):
        return pltpu.make_async_remote_copy(
            src_ref=box.at[slot],
            dst_ref=box.at[slot],
            send_sem=bulk_send.at[number],
            recv_sem=bulk_recv.at[number],
            device_id=target,
            device_id_type=LOGICAL,
        )

    def to_all(box, number):
        repeat(total, lambda k: bulk(box, number, me, device(k)).start())

    def to_column(box, number):
        repeat(rows, lambda k: bulk(box, number, i, device(k * cols)).start())

    def to_row(box, number):
        repeat(cols, lambda k: bulk(box, number, j, i * cols + lax.rem(j + k, cols)).start())

    def all_of(box, number):
        most = box.shape[0] - 1
        return pltpu.make_async_remote_copy(
            src_ref=box.at[pl.ds(0, most)],
            dst_ref=box.at[pl.ds(0, most)],
            send_sem=bulk_send.at[number],
            recv_sem=bulk_recv.at[number],
            device_id=device(1),
            device_id_type=LOGICAL,
        )

    def row_sum(field):
        part = field[:, : face // 2] + field[:, face // 2 :]
        while part.shape[1] > 128:
            part = part[:, : part.shape[1] // 2] + part[:, part.shape[1] // 2 :]
        part = jnp.concatenate([part, jnp.zeros((128 - cases, 128), F32)], axis=0)
        return jnp.sum(part.T, axis=0, keepdims=True)

    def as_column(row):
        part = jnp.broadcast_to(row, (128, 128)).T[:cases]
        return jnp.concatenate([part] * (face // 128), axis=1)

    def share_sum(number, row):
        box = sum_box.at[number]
        box[pl.ds(me, 1)] = row[None]
        to_all(box, number)

    def take_sum(number):
        box = sum_box.at[number]
        all_of(box, number).wait_recv()
        return jnp.sum(box[...], axis=0)

    sums = 2 * ITERS

    def pack(values):
        low = values.shape[0] // 2
        return jnp.concatenate([values[:low], values[low:]], axis=1)

    def unpack(values):
        values = values.astype(F32)
        return jnp.concatenate([values[:, :cases], values[:, cases:]], axis=0)

    def widen(row):
        return jnp.concatenate([row, jnp.zeros((1, 128 - cases), F32)], axis=1)

    get_loads.wait()
    for pair in PAIRS:
        for f in pair:
            get_flex[f].wait()
        for f in pair:
            out_face[0, f] = mm(loads[...], flex[f]).astype(BF16)
        if pair == PAIRS[0]:
            pl.semaphore_wait(barrier, total - 1)
        for f in pair:
            face_start(0, f)

    get_modes.wait()
    get_inverse.wait()
    for f in range(FACES):
        @pl.when(exists[f])
        def _():
            modes_copy(f, OPPOSITE[f]).start()
    if direct:
        to_column(inverse, sums)
    else:
        to_row(inverse, sums)

    get_counts.wait()
    counts = counts_ref[...].astype(F32).astype(BF16)

    def direct_table():
        span = rows * half
        lane = lax.broadcasted_iota(jnp.int32, (rows, span), 1)
        down = lax.broadcasted_iota(jnp.int32, (rows, span), 0)
        row_of = lane // half
        begin = mm(counts, jnp.where(down < row_of, 1.0, 0.0).astype(BF16))
        count = mm(counts, jnp.where(down == row_of, 1.0, 0.0).astype(BF16))
        mine = lax.broadcasted_iota(jnp.int32, (cols, span), 0) == j
        begin = jnp.sum(jnp.where(mine, begin, 0.0), axis=0, keepdims=True)
        count = jnp.sum(jnp.where(mine, count, 0.0), axis=0, keepdims=True)
        rank = lax.rem(lax.broadcasted_iota(jnp.int32, (1, span), 1), half).astype(F32)
        b = lax.broadcasted_iota(jnp.int32, (column_width, span), 0).astype(F32)
        for h in range(2):
            slot = rank + float(h * half)
            number = jnp.where(slot < count, begin + slot, -1.0)
            weight_table[pl.ds(order, column_width), pl.ds(h * span, span)] = jnp.where(
                b == number, 1.0, 0.0
            ).astype(BF16)
        all_of(inverse, sums).wait_recv()
        hot = weight_table[pl.ds(order, column_width), :]
        weight_table[pl.ds(0, order), :] = mm(
            inverse[...].reshape(order, column_width), hot
        ).astype(BF16)

    def spread_table():
        all_of(inverse, sums).wait_recv()
        tile = min(total * half, 512)
        chunk = min(column_width, 256)

        @pl.loop(0, total * half // tile)
        def _(tile_index):
            at = pl.multiple_of(tile_index * tile, tile)
            lane = at + lax.broadcasted_iota(jnp.int32, (rows, tile), 1)
            row_of = lane // (half * cols)
            down = lax.broadcasted_iota(jnp.int32, (rows, tile), 0)
            begin = mm(counts, jnp.where(down < row_of, 1.0, 0.0).astype(BF16))
            count = mm(counts, jnp.where(down == row_of, 1.0, 0.0).astype(BF16))
            lane_c = at + lax.broadcasted_iota(jnp.int32, (cols, tile), 1)
            column_of = lax.rem(lane_c // half, cols)
            which = lax.broadcasted_iota(jnp.int32, (cols, tile), 0)
            mine = which == column_of
            begin = begin + (column_of * column_width).astype(F32)
            begin = jnp.sum(jnp.where(mine, begin, 0.0), axis=0, keepdims=True)
            count = jnp.sum(jnp.where(mine, count, 0.0), axis=0, keepdims=True)
            lane_1 = at + lax.broadcasted_iota(jnp.int32, (1, tile), 1)
            rank = lax.rem(lane_1, half).astype(F32)
            for h in range(2):
                slot = rank + float(h * half)
                number = jnp.where(slot < count, begin + slot, -1.0)
                gathered = jnp.zeros((block_rows, tile), F32)
                for column in range(cols):
                    def add(c, carry, column=column, number=number):
                        first = pl.multiple_of(c * chunk, chunk)
                        down_b = lax.broadcasted_iota(jnp.int32, (chunk, tile), 0)
                        b = (down_b + (column * column_width + first)).astype(F32)
                        hot = jnp.where(b == number, 1.0, 0.0).astype(BF16)
                        return carry + mm(inverse[column, :, pl.ds(first, chunk)], hot)
                    gathered = lax.fori_loop(0, column_width // chunk, add, gathered)
                block_down = lax.broadcasted_iota(jnp.int32, (block_rows, tile), 0)
                own = (block_down + i * block_rows).astype(F32)
                weight_table[pl.ds(h * block_rows, block_rows), pl.ds(at, tile)] = gathered.astype(BF16)
                weight_table[pl.ds((2 + h) * block_rows, block_rows), pl.ds(at, tile)] = jnp.where(
                    own == number, 1.0, 0.0
                ).astype(BF16)

    if not direct:
        spread_table()

    count_f = counts_ref[...].astype(F32)
    down = lax.broadcasted_iota(jnp.int32, (cols, rows), 0)
    along = lax.broadcasted_iota(jnp.int32, (cols, rows), 1)

    def pick(row, column):
        begin = jnp.sum(
            jnp.where((down == column) & (along < row), count_f, 0.0), keepdims=True
        )
        count = jnp.sum(
            jnp.where((down == column) & (along == row), count_f, 0.0), keepdims=True
        )
        return begin + (column * column_width).astype(F32), count

    for s, (row, column) in enumerate(((i, j),) + across):
        begin, count = pick(row, column)
        rank = lax.broadcasted_iota(jnp.int32, (slots, 1), 0).astype(F32)
        number = jnp.where(rank < count, begin + rank, -1.0)
        if direct:
            lane = lax.broadcasted_iota(jnp.int32, (slots, order), 1)
            pick_table[0, pl.ds(s * slots, slots)] = jnp.where(
                lane.astype(F32) == number, 1.0, 0.0
            ).astype(BF16)
            continue
        lane = lax.broadcasted_iota(jnp.int32, (slots, rows * block_half), 1)
        for h in range(2):
            a = (lane // block_half) * block_rows + lax.rem(lane, block_half) + h * block_half
            pick_table[h, pl.ds(s * slots, slots)] = jnp.where(
                a.astype(F32) == number, 1.0, 0.0
            ).astype(BF16)

    for f in range(FACES):
        face_wait(0, f)
        r_f[f] = out_face[0, f].astype(F32) - in_face[0, f].astype(F32)

    def precondition(turn, use):
        w_box, v_box = weight_box.at[turn], value_box.at[turn]
        w_number, v_number, o_number = (sums + 1 + 3 * turn + n for n in range(3))
        weights = jnp.zeros((slots, cases), F32)
        for f in range(FACES):
            rounded = r_f[f].astype(BF16)
            weights = weights + mm_nt(modes[:, f * face : (f + 1) * face], rounded)
            moved[:, f * face : (f + 1) * face] = (rounded.astype(F32) * scale[f]).astype(BF16)
        if direct:
            w_box[pl.ds(i, 1)] = pack(weights).astype(BF16)[None]
            to_column(w_box, w_number)
        else:
            w_box[pl.ds(me, 1)] = pack(weights).astype(BF16)[None]
            to_all(w_box, w_number)

        total_f = jnp.zeros((cases, face), F32)
        for pair in PAIRS:
            for f in pair:
                if turn == 0:
                    get_dirichlet[f].wait()
            for f in pair:
                out_face[use, f] = mm(moved[...], dirichlet[f]).astype(BF16)
            for f in pair:
                face_start(use, f)
        for f in range(FACES):
            total_f = total_f + (r_f[f] * scale[f]) * out_face[use, f].astype(F32)
        row = row_sum(total_f)

        both = jnp.concatenate([row, row], axis=1)
        if direct:
            if turn > 0:
                share_sum(2 * turn, both)
            else:
                direct_table()
            all_of(w_box, w_number).wait_recv()
            out = mm(weight_table[...], unpack(w_box[...].reshape(rows * half, 2 * cases)).astype(BF16))
            v_box[pl.ds(j, 1)] = pack(out[:order])[None]
            own_box[turn, pl.ds(j, 1)] = pack(out[order:]).astype(BF16)[None]
            to_row(v_box, v_number)
            to_row(own_box.at[turn], o_number)
        else:
            all_of(w_box, w_number).wait_recv()
            out = mm(weight_table[...], w_box[...].reshape(total * half, 2 * cases))
            b = block_rows
            values = (out[:b, :cases] + out[b : 2 * b, cases:]).astype(BF16)
            own = out[2 * b : 3 * b, :cases] + out[3 * b :, cases:]
            v_box[pl.ds(i, 1)] = pack(values.astype(F32)).astype(BF16)[None]
            to_column(v_box, v_number)
            inner = jnp.sum(values.astype(F32) * own, axis=0, keepdims=True)
            row = row + widen(inner) * jnp.where(j == 0, 1.0, 0.0)
            if turn > 0:
                share_sum(2 * turn, jnp.concatenate([row, row], axis=1))

        for f in range(FACES):
            face_wait(use, f)
            local = out_face[use, f].astype(F32) - in_face[use, f].astype(F32)
            z_f[f] = local
            gz_f[f] = -local * have[f]
        if turn == 0:
            for f in range(FACES):
                @pl.when(exists[f])
                def _():
                    modes_copy(f, f).wait_recv()

        all_of(v_box, v_number).wait_recv()
        extra = jnp.zeros((1, 128), F32)
        if direct:
            all_of(own_box.at[turn], o_number).wait_recv()
            values = unpack(jnp.sum(v_box[...], axis=0)).astype(BF16)
            own = jnp.concatenate([unpack(own_box[turn, k]) for k in range(cols)], axis=0)
            extra = widen(jnp.sum(values.astype(F32) * own, axis=0, keepdims=True))
            picked = mm(pick_table[0], values)
        else:
            flat = v_box[...].reshape(rows * block_half, 2 * cases)
            picked = mm(pick_table[0], flat)[:, :cases] + mm(pick_table[1], flat)[:, cases:]
        own_picked = picked[:slots].T.astype(BF16)
        for f in range(FACES):
            z_f[f] = z_f[f] + mm(own_picked, modes[:, f * face : (f + 1) * face])
            gz_f[f] = gz_f[f] + mm_tn(picked[(1 + f) * slots : (2 + f) * slots], near_modes[f])
        return row, extra

    first_energy, extra = precondition(0, 1)
    energy = None
    use = 2
    for turn in range(ITERS):
        if turn == 0:
            for f in range(FACES):
                d_f[f] = z_f[f]
                g_f[f] = gz_f[f]
        else:
            fresh = take_sum(2 * turn)[:, :128] + extra
            beta = as_column(fresh / energy)
            energy = fresh
            for f in range(FACES):
                d_f[f] = z_f[f] + beta * d_f[f]
                g_f[f] = gz_f[f] + beta * g_f[f]
        for f in range(FACES):
            moved[:, f * face : (f + 1) * face] = (
                d_f[f].astype(BF16).astype(F32) - g_f[f].astype(BF16).astype(F32)
            ).astype(BF16)
        total_f = jnp.zeros((cases, face), F32)
        for pair in PAIRS:
            for f in pair:
                out_face[use, f] = mm(moved[...], flex[f]).astype(BF16)
            for f in pair:
                face_start(use, f)
        for f in range(FACES):
            total_f = total_f + (d_f[f] - g_f[f]) * out_face[use, f].astype(F32)
        row = row_sum(total_f)
        share_sum(2 * turn + 1, jnp.concatenate([row, first_energy], axis=1))
        for f in range(FACES):
            face_wait(use, f)
        for f in range(FACES):
            z_f[f] = out_face[use, f].astype(F32) - in_face[use, f].astype(F32)
        both = take_sum(2 * turn + 1)
        if turn == 0:
            energy = both[:, 128:] + extra
        step = as_column(energy / both[:, :128])
        for f in range(FACES):
            residual = r_f[f] - step * z_f[f]
            advance = step * d_f[f]
            if turn > 0:
                advance = x_f[f] + advance
            if turn + 1 < ITERS:
                r_f[f] = residual
                x_f[f] = advance
            else:
                mult_ref[:, f * face : (f + 1) * face] = advance.astype(BF16)
                resid_ref[:, f * face : (f + 1) * face] = residual.astype(BF16)
        use += 1
        if turn + 1 < ITERS:
            _, extra = precondition(turn + 1, use)
            use += 1

    for f in range(FACES):
        @pl.when(exists[f])
        def _():
            modes_copy(f, OPPOSITE[f]).wait_send()
            for use in range(2 * ITERS + 1):
                face_copy(use, f).wait_send()
    for number in range(1, sums):
        all_of(sum_box.at[number], number).wait_send()
    all_of(inverse, sums).wait_send()
    for turn in range(ITERS):
        all_of(weight_box.at[turn], sums + 1 + 3 * turn).wait_send()
        all_of(value_box.at[turn], sums + 2 + 3 * turn).wait_send()
        if direct:
            all_of(own_box.at[turn], sums + 3 + 3 * turn).wait_send()


def settle(mult_in, resid_in, mult_out, resid_out):
    mult_out[...] = mult_in[...]
    resid_out[...] = resid_in[...]


def shards(rows, cols, loads, flexibility, dirichlet, modes, coarse_inverse, mode_counts):
    _, _, cases, width = loads.shape
    slots = modes.shape[2]
    block_rows, column_width = coarse_inverse.shape
    total = rows * cols
    face = width // FACES
    uses = 2 * ITERS + 1
    bulks = 2 * ITERS + 1 + 3 * ITERS
    half, order = slots // 2, cols * column_width
    direct = order * column_width <= 1 << 20
    if direct:
        coarse = [
            pltpu.VMEM((order + column_width, rows * slots), BF16),
            pltpu.VMEM((1, (1 + FACES) * slots, order), BF16),
            pltpu.VMEM((ITERS, rows, half, 2 * cases), BF16),
            pltpu.VMEM((ITERS, cols, order // 2, 2 * cases), F32),
        ]
    else:
        coarse = [
            pltpu.VMEM((4 * block_rows, total * half), BF16),
            pltpu.VMEM((2, (1 + FACES) * slots, rows * block_rows // 2), BF16),
            pltpu.VMEM((ITERS, total, half, 2 * cases), BF16),
            pltpu.VMEM((ITERS, rows, block_rows // 2, 2 * cases), BF16),
        ]
    anywhere = pl.BlockSpec(memory_space=pl.ANY)
    inside = pl.BlockSpec(memory_space=pltpu.VMEM)
    field = pltpu.VMEM((FACES, cases, face), F32)
    dma = pltpu.SemaphoreType.DMA
    mult, resid = pl.pallas_call(
        functools.partial(kernel, rows, cols, direct),
        out_shape=[jax.ShapeDtypeStruct((cases, width), BF16)] * 2,
        in_specs=[anywhere] * 6,
        out_specs=[inside] * 2,
        scratch_shapes=[
            pltpu.VMEM((cases, width), BF16),
            pltpu.VMEM((FACES, width, face), BF16),
            pltpu.VMEM((FACES, width, face), BF16),
            pltpu.VMEM((slots, width), BF16),
            pltpu.VMEM((rows if direct else cols, block_rows, column_width), BF16),
            pltpu.VMEM((cols, rows), jnp.int32),
            pltpu.VMEM((FACES, slots, face), BF16),
            *coarse,
            pltpu.VMEM((ITERS, cols, column_width // 2, 2 * cases), BF16),
            pltpu.VMEM((2 * ITERS, total, 1, 256), F32),
            pltpu.VMEM((uses, FACES, cases, face), BF16),
            pltpu.VMEM((uses, FACES, cases, face), BF16),
            pltpu.VMEM((cases, width), BF16),
            field, field, field, field, field, field,
            dma((12,)),
            dma((uses, FACES)),
            dma((uses, FACES)),
            dma((FACES,)),
            dma((FACES,)),
            dma((bulks,)),
            dma((bulks,)),
        ],
        compiler_params=pltpu.CompilerParams(
            collective_id=0, has_side_effects=True, vmem_limit_bytes=62 * 1024 * 1024
        ),
    )(
        loads.reshape(cases, width),
        flexibility.reshape(width, width),
        dirichlet.reshape(width, width),
        modes.reshape(slots, width),
        coarse_inverse,
        mode_counts,
    )
    mult, resid = pl.pallas_call(
        settle,
        out_shape=[jax.ShapeDtypeStruct((cases, width), BF16)] * 2,
        in_specs=[inside] * 2,
        out_specs=[inside] * 2,
        compiler_params=pltpu.CompilerParams(vmem_limit_bytes=62 * 1024 * 1024),
    )(mult, resid)
    return mult[None, None], resid[None, None]


def solution(mesh):
    return jax.shard_map(
        functools.partial(shards, mesh.shape["wide"], mesh.shape["narrow"]),
        mesh=mesh,
        in_specs=(
            P("wide", "narrow", None, None),
            P("wide", "narrow", None, None),
            P("wide", "narrow", None, None),
            P("wide", "narrow", None, None),
            P("wide", "narrow"),
            P(),
        ),
        out_specs=(P("wide", "narrow", None, None), P("wide", "narrow", None, None)),
        check_vma=False,
    )
```

```python
import functools

import jax
import jax.numpy as jnp
from jax import lax
from jax.experimental import pallas as pl
from jax.experimental.pallas import tpu as pltpu
from jax.sharding import PartitionSpec as P

MESH = pl.DeviceIdType.MESH
LOGICAL = pl.DeviceIdType.LOGICAL
ITERS = 2
FACES = 4
OPPOSITE = (1, 0, 3, 2)
PAIRS = ((0, 1), (2, 3))
F32 = jnp.float32
BF16 = jnp.bfloat16


def mm(left, right):
    return jnp.dot(left, right, preferred_element_type=F32)


def mm_nt(left, right):
    return lax.dot_general(left, right, (((1,), (1,)), ((), ())), preferred_element_type=F32)


def mm_tn(left, right):
    return mm(left.T.astype(BF16), right)


def kernel(
    rows, cols, direct, loads_hbm, flex_hbm, dirichlet_hbm, modes_hbm, inverse_hbm, counts_hbm,
    mult_ref, resid_ref,
    loads, flex, dirichlet, modes, inverse, counts_ref, near_modes, weight_table, pick_table,
    weight_box, value_box, own_box, sum_box, out_face, in_face, moved, r_f, d_f, g_f, z_f, gz_f, x_f,
    load_sem, face_send, face_recv, setup_send, setup_recv, bulk_send, bulk_recv,
):
    total = rows * cols
    i = lax.axis_index("wide")
    j = lax.axis_index("narrow")
    me = i * cols + j
    cases = loads.shape[0]
    face = loads.shape[1] // FACES
    slots = modes.shape[0]
    half = slots // 2
    block_rows, column_width = inverse.shape[1], inverse.shape[2]
    block_half = block_rows // 2
    order = cols * column_width

    exists = (i > 0, i < rows - 1, j > 0, j < cols - 1)
    across = ((i - 1, j), (i + 1, j), (i, j - 1), (i, j + 1))
    have = [jnp.where(e, 1.0, 0.0).astype(F32) for e in exists]
    scale = [1.0 + h for h in have]

    def device(k):
        return lax.rem(me + k, total)

    def repeat(last, body):
        if last <= 64:
            for k in sorted(range(1, last), key=lambda k: abs(2 * k - last)):
                body(k)
        else:
            pl.loop(1, last)(body)

    def fetch(source, target, number):
        copy = pltpu.make_async_copy(source, target, load_sem.at[number])
        copy.start()
        return copy

    get_loads = fetch(loads_hbm, loads, 0)
    get_flex = [
        fetch(flex_hbm.at[:, pl.ds(f * face, face)], flex.at[f], 1 + f) for f in range(FACES)
    ]
    barrier = pltpu.get_barrier_semaphore()

    def greet(k):
        pl.semaphore_signal(barrier, inc=1, device_id=device(k), device_id_type=LOGICAL)

    repeat(total, greet)

    get_modes = fetch(modes_hbm, modes, 9)
    get_inverse = fetch(inverse_hbm, inverse.at[i if direct else j], 10)
    get_counts = fetch(counts_hbm, counts_ref, 11)
    get_dirichlet = [
        fetch(dirichlet_hbm.at[:, pl.ds(f * face, face)], dirichlet.at[f], 5 + f)
        for f in range(FACES)
    ]

    for f in range(FACES):
        @pl.when(jnp.logical_not(exists[f]))
        def _():
            in_face[:, f] = jnp.zeros((in_face.shape[0], cases, face), BF16)
            near_modes[f] = jnp.zeros((slots, face), BF16)

    def face_copy(use, f):
        return pltpu.make_async_remote_copy(
            src_ref=out_face.at[use, f],
            dst_ref=in_face.at[use, OPPOSITE[f]],
            send_sem=face_send.at[use, f],
            recv_sem=face_recv.at[use, OPPOSITE[f]],
            device_id=across[f],
            device_id_type=MESH,
        )

    def face_start(use, f):
        @pl.when(exists[f])
        def _():
            face_copy(use, f).start()

    def face_wait(use, f):
        @pl.when(exists[f])
        def _():
            pltpu.make_async_remote_copy(
                src_ref=out_face.at[use, f],
                dst_ref=in_face.at[use, f],
                send_sem=face_send.at[use, f],
                recv_sem=face_recv.at[use, f],
                device_id=across[f],
                device_id_type=MESH,
            ).wait_recv()

    def modes_copy(f, slot):
        return pltpu.make_async_remote_copy(
            src_ref=modes.at[:, pl.ds(f * face, face)],
            dst_ref=near_modes.at[slot],
            send_sem=setup_send.at[f],
            recv_sem=setup_recv.at[slot],
            device_id=across[f],
            device_id_type=MESH,
        )

    def bulk(box, number, slot, target):
        return pltpu.make_async_remote_copy(
            src_ref=box.at[slot],
            dst_ref=box.at[slot],
            send_sem=bulk_send.at[number],
            recv_sem=bulk_recv.at[number],
            device_id=target,
            device_id_type=LOGICAL,
        )

    def to_all(box, number):
        repeat(total, lambda k: bulk(box, number, me, device(k)).start())

    def to_column(box, number):
        repeat(rows, lambda k: bulk(box, number, i, device(k * cols)).start())

    def to_row(box, number):
        repeat(cols, lambda k: bulk(box, number, j, i * cols + lax.rem(j + k, cols)).start())

    def all_of(box, number):
        most = box.shape[0] - 1
        return pltpu.make_async_remote_copy(
            src_ref=box.at[pl.ds(0, most)],
            dst_ref=box.at[pl.ds(0, most)],
            send_sem=bulk_send.at[number],
            recv_sem=bulk_recv.at[number],
            device_id=device(1),
            device_id_type=LOGICAL,
        )

    def row_sum(field):
        part = field[:, : face // 2] + field[:, face // 2 :]
        while part.shape[1] > 128:
            part = part[:, : part.shape[1] // 2] + part[:, part.shape[1] // 2 :]
        part = jnp.concatenate([part, jnp.zeros((128 - cases, 128), F32)], axis=0)
        return jnp.sum(part.T, axis=0, keepdims=True)

    def as_column(row):
        part = jnp.broadcast_to(row, (128, 128)).T[:cases]
        return jnp.concatenate([part] * (face // 128), axis=1)

    def share_sum(number, row):
        box = sum_box.at[number]
        box[pl.ds(me, 1)] = row[None]
        to_all(box, number)

    def take_sum(number):
        box = sum_box.at[number]
        all_of(box, number).wait_recv()
        return jnp.sum(box[...], axis=0)

    sums = 2 * ITERS

    def pack(values):
        low = values.shape[0] // 2
        return jnp.concatenate([values[:low], values[low:]], axis=1)

    def unpack(values):
        values = values.astype(F32)
        return jnp.concatenate([values[:, :cases], values[:, cases:]], axis=0)

    def widen(row):
        return jnp.concatenate([row, jnp.zeros((1, 128 - cases), F32)], axis=1)

    get_loads.wait()
    for pair in PAIRS:
        for f in pair:
            get_flex[f].wait()
        for f in pair:
            out_face[0, f] = mm(loads[...], flex[f]).astype(BF16)
        if pair == PAIRS[0]:
            pl.semaphore_wait(barrier, total - 1)
        for f in pair:
            face_start(0, f)

    get_modes.wait()
    get_inverse.wait()
    for f in range(FACES):
        @pl.when(exists[f])
        def _():
            modes_copy(f, OPPOSITE[f]).start()
    if direct:
        to_column(inverse, sums)
    else:
        to_row(inverse, sums)

    get_counts.wait()
    counts = counts_ref[...].astype(F32).astype(BF16)

    def direct_table():
        span = rows * half
        lane = lax.broadcasted_iota(jnp.int32, (rows, span), 1)
        down = lax.broadcasted_iota(jnp.int32, (rows, span), 0)
        row_of = lane // half
        begin = mm(counts, jnp.where(down < row_of, 1.0, 0.0).astype(BF16))
        count = mm(counts, jnp.where(down == row_of, 1.0, 0.0).astype(BF16))
        mine = lax.broadcasted_iota(jnp.int32, (cols, span), 0) == j
        begin = jnp.sum(jnp.where(mine, begin, 0.0), axis=0, keepdims=True)
        count = jnp.sum(jnp.where(mine, count, 0.0), axis=0, keepdims=True)
        rank = lax.rem(lax.broadcasted_iota(jnp.int32, (1, span), 1), half).astype(F32)
        b = lax.broadcasted_iota(jnp.int32, (column_width, span), 0).astype(F32)
        for h in range(2):
            slot = rank + float(h * half)
            number = jnp.where(slot < count, begin + slot, -1.0)
            weight_table[pl.ds(order, column_width), pl.ds(h * span, span)] = jnp.where(
                b == number, 1.0, 0.0
            ).astype(BF16)
        all_of(inverse, sums).wait_recv()
        hot = weight_table[pl.ds(order, column_width), :]
        weight_table[pl.ds(0, order), :] = mm(
            inverse[...].reshape(order, column_width), hot
        ).astype(BF16)

    def spread_table():
        all_of(inverse, sums).wait_recv()
        tile = min(total * half, 512)
        chunk = min(column_width, 256)

        @pl.loop(0, total * half // tile)
        def _(tile_index):
            at = pl.multiple_of(tile_index * tile, tile)
            lane = at + lax.broadcasted_iota(jnp.int32, (rows, tile), 1)
            row_of = lane // (half * cols)
            down = lax.broadcasted_iota(jnp.int32, (rows, tile), 0)
            begin = mm(counts, jnp.where(down < row_of, 1.0, 0.0).astype(BF16))
            count = mm(counts, jnp.where(down == row_of, 1.0, 0.0).astype(BF16))
            lane_c = at + lax.broadcasted_iota(jnp.int32, (cols, tile), 1)
            column_of = lax.rem(lane_c // half, cols)
            which = lax.broadcasted_iota(jnp.int32, (cols, tile), 0)
            mine = which == column_of
            begin = begin + (column_of * column_width).astype(F32)
            begin = jnp.sum(jnp.where(mine, begin, 0.0), axis=0, keepdims=True)
            count = jnp.sum(jnp.where(mine, count, 0.0), axis=0, keepdims=True)
            lane_1 = at + lax.broadcasted_iota(jnp.int32, (1, tile), 1)
            rank = lax.rem(lane_1, half).astype(F32)
            for h in range(2):
                slot = rank + float(h * half)
                number = jnp.where(slot < count, begin + slot, -1.0)
                gathered = jnp.zeros((block_rows, tile), F32)
                for column in range(cols):
                    def add(c, carry, column=column, number=number):
                        first = pl.multiple_of(c * chunk, chunk)
                        down_b = lax.broadcasted_iota(jnp.int32, (chunk, tile), 0)
                        b = (down_b + (column * column_width + first)).astype(F32)
                        hot = jnp.where(b == number, 1.0, 0.0).astype(BF16)
                        return carry + mm(inverse[column, :, pl.ds(first, chunk)], hot)
                    gathered = lax.fori_loop(0, column_width // chunk, add, gathered)
                block_down = lax.broadcasted_iota(jnp.int32, (block_rows, tile), 0)
                own = (block_down + i * block_rows).astype(F32)
                weight_table[pl.ds(h * block_rows, block_rows), pl.ds(at, tile)] = gathered.astype(BF16)
                weight_table[pl.ds((2 + h) * block_rows, block_rows), pl.ds(at, tile)] = jnp.where(
                    own == number, 1.0, 0.0
                ).astype(BF16)

    if not direct:
        spread_table()

    count_f = counts_ref[...].astype(F32)
    down = lax.broadcasted_iota(jnp.int32, (cols, rows), 0)
    along = lax.broadcasted_iota(jnp.int32, (cols, rows), 1)

    def pick(row, column):
        begin = jnp.sum(
            jnp.where((down == column) & (along < row), count_f, 0.0), keepdims=True
        )
        count = jnp.sum(
            jnp.where((down == column) & (along == row), count_f, 0.0), keepdims=True
        )
        return begin + (column * column_width).astype(F32), count

    for s, (row, column) in enumerate(((i, j),) + across):
        begin, count = pick(row, column)
        rank = lax.broadcasted_iota(jnp.int32, (slots, 1), 0).astype(F32)
        number = jnp.where(rank < count, begin + rank, -1.0)
        if direct:
            lane = lax.broadcasted_iota(jnp.int32, (slots, order), 1)
            pick_table[0, pl.ds(s * slots, slots)] = jnp.where(
                lane.astype(F32) == number, 1.0, 0.0
            ).astype(BF16)
            continue
        lane = lax.broadcasted_iota(jnp.int32, (slots, rows * block_half), 1)
        for h in range(2):
            a = (lane // block_half) * block_rows + lax.rem(lane, block_half) + h * block_half
            pick_table[h, pl.ds(s * slots, slots)] = jnp.where(
                a.astype(F32) == number, 1.0, 0.0
            ).astype(BF16)

    for f in range(FACES):
        face_wait(0, f)
        r_f[f] = out_face[0, f].astype(F32) - in_face[0, f].astype(F32)

    def precondition(turn, use):
        w_box, v_box = weight_box.at[turn], value_box.at[turn]
        w_number, v_number, o_number = (sums + 1 + 3 * turn + n for n in range(3))
        weights = jnp.zeros((slots, cases), F32)
        for f in range(FACES):
            rounded = r_f[f].astype(BF16)
            weights = weights + mm_nt(modes[:, f * face : (f + 1) * face], rounded)
            moved[:, f * face : (f + 1) * face] = (rounded.astype(F32) * scale[f]).astype(BF16)
        if direct:
            w_box[pl.ds(i, 1)] = pack(weights).astype(BF16)[None]
            to_column(w_box, w_number)
        else:
            w_box[pl.ds(me, 1)] = pack(weights).astype(BF16)[None]
            to_all(w_box, w_number)

        total_f = jnp.zeros((cases, face), F32)
        for pair in PAIRS:
            for f in pair:
                if turn == 0:
                    get_dirichlet[f].wait()
            for f in pair:
                out_face[use, f] = mm(moved[...], dirichlet[f]).astype(BF16)
            for f in pair:
                face_start(use, f)
        for f in range(FACES):
            total_f = total_f + (r_f[f] * scale[f]) * out_face[use, f].astype(F32)
        row = row_sum(total_f)

        both = jnp.concatenate([row, row], axis=1)
        if direct:
            if turn > 0:
                share_sum(2 * turn, both)
            else:
                direct_table()
            all_of(w_box, w_number).wait_recv()
            out = mm(weight_table[...], unpack(w_box[...].reshape(rows * half, 2 * cases)).astype(BF16))
            v_box[pl.ds(j, 1)] = pack(out[:order])[None]
            own_box[turn, pl.ds(j, 1)] = pack(out[order:]).astype(BF16)[None]
            to_row(v_box, v_number)
            to_row(own_box.at[turn], o_number)
        else:
            all_of(w_box, w_number).wait_recv()
            out = mm(weight_table[...], w_box[...].reshape(total * half, 2 * cases))
            b = block_rows
            values = (out[:b, :cases] + out[b : 2 * b, cases:]).astype(BF16)
            own = out[2 * b : 3 * b, :cases] + out[3 * b :, cases:]
            v_box[pl.ds(i, 1)] = pack(values.astype(F32)).astype(BF16)[None]
            to_column(v_box, v_number)
            inner = jnp.sum(values.astype(F32) * own, axis=0, keepdims=True)
            row = row + widen(inner) * jnp.where(j == 0, 1.0, 0.0)
            if turn > 0:
                share_sum(2 * turn, jnp.concatenate([row, row], axis=1))

        for f in range(FACES):
            face_wait(use, f)
            local = out_face[use, f].astype(F32) - in_face[use, f].astype(F32)
            z_f[f] = local
            gz_f[f] = -local * have[f]
        if turn == 0:
            for f in range(FACES):
                @pl.when(exists[f])
                def _():
                    modes_copy(f, f).wait_recv()

        all_of(v_box, v_number).wait_recv()
        extra = jnp.zeros((1, 128), F32)
        if direct:
            all_of(own_box.at[turn], o_number).wait_recv()
            values = unpack(jnp.sum(v_box[...], axis=0)).astype(BF16)
            own = jnp.concatenate([unpack(own_box[turn, k]) for k in range(cols)], axis=0)
            extra = widen(jnp.sum(values.astype(F32) * own, axis=0, keepdims=True))
            picked = mm(pick_table[0], values)
        else:
            flat = v_box[...].reshape(rows * block_half, 2 * cases)
            picked = mm(pick_table[0], flat)[:, :cases] + mm(pick_table[1], flat)[:, cases:]
        own_picked = picked[:slots].T.astype(BF16)
        for f in range(FACES):
            z_f[f] = z_f[f] + mm(own_picked, modes[:, f * face : (f + 1) * face])
            gz_f[f] = gz_f[f] + mm_tn(picked[(1 + f) * slots : (2 + f) * slots], near_modes[f])
        return row, extra

    first_energy, extra = precondition(0, 1)
    energy = None
    use = 2
    for turn in range(ITERS):
        if turn == 0:
            for f in range(FACES):
                d_f[f] = z_f[f]
                g_f[f] = gz_f[f]
        else:
            fresh = take_sum(2 * turn)[:, :128] + extra
            beta = as_column(fresh / energy)
            energy = fresh
            for f in range(FACES):
                d_f[f] = z_f[f] + beta * d_f[f]
                g_f[f] = gz_f[f] + beta * g_f[f]
        for f in range(FACES):
            moved[:, f * face : (f + 1) * face] = (
                d_f[f].astype(BF16).astype(F32) - g_f[f].astype(BF16).astype(F32)
            ).astype(BF16)
        total_f = jnp.zeros((cases, face), F32)
        for f in range(FACES):
            image = mm(moved[...], flex[f]).astype(BF16)
            out_face[use, f] = image
            total_f = total_f + (d_f[f] - g_f[f]) * image.astype(F32)
        row = row_sum(total_f)
        for f in PAIRS[0]:
            face_start(use, f)
        share_sum(2 * turn + 1, jnp.concatenate([row, first_energy], axis=1))
        for f in PAIRS[1]:
            face_start(use, f)
        for f in range(FACES):
            face_wait(use, f)
        for f in range(FACES):
            z_f[f] = out_face[use, f].astype(F32) - in_face[use, f].astype(F32)
        both = take_sum(2 * turn + 1)
        if turn == 0:
            energy = both[:, 128:] + extra
        step = as_column(energy / both[:, :128])
        for f in range(FACES):
            residual = r_f[f] - step * z_f[f]
            advance = step * d_f[f]
            if turn > 0:
                advance = x_f[f] + advance
            if turn + 1 < ITERS:
                r_f[f] = residual
                x_f[f] = advance
            else:
                mult_ref[:, f * face : (f + 1) * face] = advance.astype(BF16)
                resid_ref[:, f * face : (f + 1) * face] = residual.astype(BF16)
        use += 1
        if turn + 1 < ITERS:
            _, extra = precondition(turn + 1, use)
            use += 1

    for f in range(FACES):
        @pl.when(exists[f])
        def _():
            modes_copy(f, OPPOSITE[f]).wait_send()
            for use in range(2 * ITERS + 1):
                face_copy(use, f).wait_send()
    for number in range(1, sums):
        all_of(sum_box.at[number], number).wait_send()
    all_of(inverse, sums).wait_send()
    for turn in range(ITERS):
        all_of(weight_box.at[turn], sums + 1 + 3 * turn).wait_send()
        all_of(value_box.at[turn], sums + 2 + 3 * turn).wait_send()
        if direct:
            all_of(own_box.at[turn], sums + 3 + 3 * turn).wait_send()


def settle(mult_in, resid_in, mult_out, resid_out):
    mult_out[...] = mult_in[...]
    resid_out[...] = resid_in[...]


def shards(rows, cols, loads, flexibility, dirichlet, modes, coarse_inverse, mode_counts):
    _, _, cases, width = loads.shape
    slots = modes.shape[2]
    block_rows, column_width = coarse_inverse.shape
    total = rows * cols
    face = width // FACES
    uses = 2 * ITERS + 1
    bulks = 2 * ITERS + 1 + 3 * ITERS
    half, order = slots // 2, cols * column_width
    direct = order * column_width <= 1 << 20
    if direct:
        coarse = [
            pltpu.VMEM((order + column_width, rows * slots), BF16),
            pltpu.VMEM((1, (1 + FACES) * slots, order), BF16),
            pltpu.VMEM((ITERS, rows, half, 2 * cases), BF16),
            pltpu.VMEM((ITERS, cols, order // 2, 2 * cases), F32),
        ]
    else:
        coarse = [
            pltpu.VMEM((4 * block_rows, total * half), BF16),
            pltpu.VMEM((2, (1 + FACES) * slots, rows * block_rows // 2), BF16),
            pltpu.VMEM((ITERS, total, half, 2 * cases), BF16),
            pltpu.VMEM((ITERS, rows, block_rows // 2, 2 * cases), BF16),
        ]
    anywhere = pl.BlockSpec(memory_space=pl.ANY)
    inside = pl.BlockSpec(memory_space=pltpu.VMEM)
    field = pltpu.VMEM((FACES, cases, face), F32)
    dma = pltpu.SemaphoreType.DMA
    mult, resid = pl.pallas_call(
        functools.partial(kernel, rows, cols, direct),
        out_shape=[jax.ShapeDtypeStruct((cases, width), BF16)] * 2,
        in_specs=[anywhere] * 6,
        out_specs=[inside] * 2,
        scratch_shapes=[
            pltpu.VMEM((cases, width), BF16),
            pltpu.VMEM((FACES, width, face), BF16),
            pltpu.VMEM((FACES, width, face), BF16),
            pltpu.VMEM((slots, width), BF16),
            pltpu.VMEM((rows if direct else cols, block_rows, column_width), BF16),
            pltpu.VMEM((cols, rows), jnp.int32),
            pltpu.VMEM((FACES, slots, face), BF16),
            *coarse,
            pltpu.VMEM((ITERS, cols, column_width // 2, 2 * cases), BF16),
            pltpu.VMEM((2 * ITERS, total, 1, 256), F32),
            pltpu.VMEM((uses, FACES, cases, face), BF16),
            pltpu.VMEM((uses, FACES, cases, face), BF16),
            pltpu.VMEM((cases, width), BF16),
            field, field, field, field, field, field,
            dma((12,)),
            dma((uses, FACES)),
            dma((uses, FACES)),
            dma((FACES,)),
            dma((FACES,)),
            dma((bulks,)),
            dma((bulks,)),
        ],
        compiler_params=pltpu.CompilerParams(
            collective_id=0, has_side_effects=True, vmem_limit_bytes=62 * 1024 * 1024
        ),
    )(
        loads.reshape(cases, width),
        flexibility.reshape(width, width),
        dirichlet.reshape(width, width),
        modes.reshape(slots, width),
        coarse_inverse,
        mode_counts,
    )
    mult, resid = pl.pallas_call(
        settle,
        out_shape=[jax.ShapeDtypeStruct((cases, width), BF16)] * 2,
        in_specs=[inside] * 2,
        out_specs=[inside] * 2,
        compiler_params=pltpu.CompilerParams(vmem_limit_bytes=62 * 1024 * 1024),
    )(mult, resid)
    return mult[None, None], resid[None, None]


def solution(mesh):
    return jax.shard_map(
        functools.partial(shards, mesh.shape["wide"], mesh.shape["narrow"]),
        mesh=mesh,
        in_specs=(
            P("wide", "narrow", None, None),
            P("wide", "narrow", None, None),
            P("wide", "narrow", None, None),
            P("wide", "narrow", None, None),
            P("wide", "narrow"),
            P(),
        ),
        out_specs=(P("wide", "narrow", None, None), P("wide", "narrow", None, None)),
        check_vma=False,
    )
```

```python
import functools

import jax
import jax.numpy as jnp
from jax import lax
from jax.experimental import pallas as pl
from jax.experimental.pallas import tpu as pltpu
from jax.sharding import PartitionSpec as P

MESH = pl.DeviceIdType.MESH
LOGICAL = pl.DeviceIdType.LOGICAL
ITERS = 2
FACES = 4
OPPOSITE = (1, 0, 3, 2)
PAIRS = ((0, 1), (2, 3))
F32 = jnp.float32
BF16 = jnp.bfloat16


def mm(left, right):
    return jnp.dot(left, right, preferred_element_type=F32)


def mm_nt(left, right):
    return lax.dot_general(left, right, (((1,), (1,)), ((), ())), preferred_element_type=F32)


def mm_tn(left, right):
    return mm(left.T.astype(BF16), right)


def kernel(
    rows, cols, direct, loads_hbm, flex_hbm, dirichlet_hbm, modes_hbm, inverse_hbm, counts_hbm,
    mult_ref, resid_ref,
    loads, flex, dirichlet, modes, inverse, counts_ref, near_modes, weight_table, pick_table,
    weight_box, value_box, own_box, sum_box, out_face, in_face, moved, r_f, d_f, g_f, z_f, gz_f, x_f,
    load_sem, face_send, face_recv, setup_send, setup_recv, bulk_send, bulk_recv,
):
    total = rows * cols
    i = lax.axis_index("wide")
    j = lax.axis_index("narrow")
    me = i * cols + j
    cases = loads.shape[0]
    face = loads.shape[1] // FACES
    slots = modes.shape[0]
    half = slots // 2
    block_rows, column_width = inverse.shape[1], inverse.shape[2]
    block_half = block_rows // 2
    order = cols * column_width

    exists = (i > 0, i < rows - 1, j > 0, j < cols - 1)
    across = ((i - 1, j), (i + 1, j), (i, j - 1), (i, j + 1))
    have = [jnp.where(e, 1.0, 0.0).astype(F32) for e in exists]
    scale = [1.0 + h for h in have]

    def device(k):
        return lax.rem(me + k, total)

    def repeat(last, body):
        if last <= 64:
            for k in sorted(range(1, last), key=lambda k: abs(2 * k - last)):
                body(k)
        else:
            pl.loop(1, last)(body)

    def fetch(source, target, number):
        copy = pltpu.make_async_copy(source, target, load_sem.at[number])
        copy.start()
        return copy

    get_loads = fetch(loads_hbm, loads, 0)
    get_flex = [
        fetch(flex_hbm.at[:, pl.ds(f * face, face)], flex.at[f], 1 + f) for f in range(FACES)
    ]
    barrier = pltpu.get_barrier_semaphore()

    def greet(k):
        pl.semaphore_signal(barrier, inc=1, device_id=device(k), device_id_type=LOGICAL)

    repeat(total, greet)

    get_modes = fetch(modes_hbm, modes, 9)
    get_inverse = fetch(inverse_hbm, inverse.at[i if direct else j], 10)
    get_counts = fetch(counts_hbm, counts_ref, 11)
    get_dirichlet = [
        fetch(dirichlet_hbm.at[:, pl.ds(f * face, face)], dirichlet.at[f], 5 + f)
        for f in range(FACES)
    ]

    for f in range(FACES):
        @pl.when(jnp.logical_not(exists[f]))
        def _():
            in_face[:, f] = jnp.zeros((in_face.shape[0], cases, face), BF16)
            near_modes[f] = jnp.zeros((slots, face), BF16)

    def face_copy(use, f):
        return pltpu.make_async_remote_copy(
            src_ref=out_face.at[use, f],
            dst_ref=in_face.at[use, OPPOSITE[f]],
            send_sem=face_send.at[use, f],
            recv_sem=face_recv.at[use, OPPOSITE[f]],
            device_id=across[f],
            device_id_type=MESH,
        )

    def face_start(use, f):
        @pl.when(exists[f])
        def _():
            face_copy(use, f).start()

    def face_wait(use, f):
        @pl.when(exists[f])
        def _():
            pltpu.make_async_remote_copy(
                src_ref=out_face.at[use, f],
                dst_ref=in_face.at[use, f],
                send_sem=face_send.at[use, f],
                recv_sem=face_recv.at[use, f],
                device_id=across[f],
                device_id_type=MESH,
            ).wait_recv()

    def modes_copy(f, slot):
        return pltpu.make_async_remote_copy(
            src_ref=modes.at[:, pl.ds(f * face, face)],
            dst_ref=near_modes.at[slot],
            send_sem=setup_send.at[f],
            recv_sem=setup_recv.at[slot],
            device_id=across[f],
            device_id_type=MESH,
        )

    def bulk(box, number, slot, target):
        return pltpu.make_async_remote_copy(
            src_ref=box.at[slot],
            dst_ref=box.at[slot],
            send_sem=bulk_send.at[number],
            recv_sem=bulk_recv.at[number],
            device_id=target,
            device_id_type=LOGICAL,
        )

    def to_all(box, number):
        repeat(total, lambda k: bulk(box, number, me, device(k)).start())

    def to_column(box, number):
        repeat(rows, lambda k: bulk(box, number, i, device(k * cols)).start())

    def to_row(box, number):
        repeat(cols, lambda k: bulk(box, number, j, i * cols + lax.rem(j + k, cols)).start())

    def all_of(box, number):
        most = box.shape[0] - 1
        return pltpu.make_async_remote_copy(
            src_ref=box.at[pl.ds(0, most)],
            dst_ref=box.at[pl.ds(0, most)],
            send_sem=bulk_send.at[number],
            recv_sem=bulk_recv.at[number],
            device_id=device(1),
            device_id_type=LOGICAL,
        )

    def row_sum(field):
        part = field[:, : face // 2] + field[:, face // 2 :]
        while part.shape[1] > 128:
            part = part[:, : part.shape[1] // 2] + part[:, part.shape[1] // 2 :]
        part = jnp.concatenate([part, jnp.zeros((128 - cases, 128), F32)], axis=0)
        return jnp.sum(part.T, axis=0, keepdims=True)

    def as_column(row):
        part = jnp.broadcast_to(row, (128, 128)).T[:cases]
        return jnp.concatenate([part] * (face // 128), axis=1)

    def share_sum(number, row):
        box = sum_box.at[number]
        box[pl.ds(me, 1)] = row[None]
        to_all(box, number)

    def take_sum(number):
        box = sum_box.at[number]
        all_of(box, number).wait_recv()
        return jnp.sum(box[...], axis=0)

    sums = 2 * ITERS

    def pack(values):
        low = values.shape[0] // 2
        return jnp.concatenate([values[:low], values[low:]], axis=1)

    def unpack(values):
        values = values.astype(F32)
        return jnp.concatenate([values[:, :cases], values[:, cases:]], axis=0)

    def widen(row):
        return jnp.concatenate([row, jnp.zeros((1, 128 - cases), F32)], axis=1)

    get_loads.wait()
    for pair in PAIRS:
        for f in pair:
            get_flex[f].wait()
        for f in pair:
            out_face[0, f] = mm(loads[...], flex[f]).astype(BF16)
        if pair == PAIRS[0]:
            pl.semaphore_wait(barrier, total - 1)
        for f in pair:
            face_start(0, f)
        if pair == PAIRS[0]:
            get_modes.wait()
            get_inverse.wait()
            for f in range(FACES):
                @pl.when(exists[f])
                def _(f=f):
                    modes_copy(f, OPPOSITE[f]).start()
            if direct:
                to_column(inverse, sums)
            else:
                to_row(inverse, sums)


    get_counts.wait()
    counts = counts_ref[...].astype(F32).astype(BF16)

    def direct_table():
        span = rows * half
        lane = lax.broadcasted_iota(jnp.int32, (rows, span), 1)
        down = lax.broadcasted_iota(jnp.int32, (rows, span), 0)
        row_of = lane // half
        begin = mm(counts, jnp.where(down < row_of, 1.0, 0.0).astype(BF16))
        count = mm(counts, jnp.where(down == row_of, 1.0, 0.0).astype(BF16))
        mine = lax.broadcasted_iota(jnp.int32, (cols, span), 0) == j
        begin = jnp.sum(jnp.where(mine, begin, 0.0), axis=0, keepdims=True)
        count = jnp.sum(jnp.where(mine, count, 0.0), axis=0, keepdims=True)
        rank = lax.rem(lax.broadcasted_iota(jnp.int32, (1, span), 1), half).astype(F32)
        b = lax.broadcasted_iota(jnp.int32, (column_width, span), 0).astype(F32)
        for h in range(2):
            slot = rank + float(h * half)
            number = jnp.where(slot < count, begin + slot, -1.0)
            weight_table[pl.ds(order, column_width), pl.ds(h * span, span)] = jnp.where(
                b == number, 1.0, 0.0
            ).astype(BF16)
        all_of(inverse, sums).wait_recv()
        hot = weight_table[pl.ds(order, column_width), :]
        weight_table[pl.ds(0, order), :] = mm(
            inverse[...].reshape(order, column_width), hot
        ).astype(BF16)

    def spread_table():
        all_of(inverse, sums).wait_recv()
        tile = min(total * half, 512)
        chunk = min(column_width, 256)

        @pl.loop(0, total * half // tile)
        def _(tile_index):
            at = pl.multiple_of(tile_index * tile, tile)
            lane = at + lax.broadcasted_iota(jnp.int32, (rows, tile), 1)
            row_of = lane // (half * cols)
            down = lax.broadcasted_iota(jnp.int32, (rows, tile), 0)
            begin = mm(counts, jnp.where(down < row_of, 1.0, 0.0).astype(BF16))
            count = mm(counts, jnp.where(down == row_of, 1.0, 0.0).astype(BF16))
            lane_c = at + lax.broadcasted_iota(jnp.int32, (cols, tile), 1)
            column_of = lax.rem(lane_c // half, cols)
            which = lax.broadcasted_iota(jnp.int32, (cols, tile), 0)
            mine = which == column_of
            begin = begin + (column_of * column_width).astype(F32)
            begin = jnp.sum(jnp.where(mine, begin, 0.0), axis=0, keepdims=True)
            count = jnp.sum(jnp.where(mine, count, 0.0), axis=0, keepdims=True)
            lane_1 = at + lax.broadcasted_iota(jnp.int32, (1, tile), 1)
            rank = lax.rem(lane_1, half).astype(F32)
            for h in range(2):
                slot = rank + float(h * half)
                number = jnp.where(slot < count, begin + slot, -1.0)
                gathered = jnp.zeros((block_rows, tile), F32)
                for column in range(cols):
                    def add(c, carry, column=column, number=number):
                        first = pl.multiple_of(c * chunk, chunk)
                        down_b = lax.broadcasted_iota(jnp.int32, (chunk, tile), 0)
                        b = (down_b + (column * column_width + first)).astype(F32)
                        hot = jnp.where(b == number, 1.0, 0.0).astype(BF16)
                        return carry + mm(inverse[column, :, pl.ds(first, chunk)], hot)
                    gathered = lax.fori_loop(0, column_width // chunk, add, gathered)
                block_down = lax.broadcasted_iota(jnp.int32, (block_rows, tile), 0)
                own = (block_down + i * block_rows).astype(F32)
                weight_table[pl.ds(h * block_rows, block_rows), pl.ds(at, tile)] = gathered.astype(BF16)
                weight_table[pl.ds((2 + h) * block_rows, block_rows), pl.ds(at, tile)] = jnp.where(
                    own == number, 1.0, 0.0
                ).astype(BF16)

    if not direct:
        spread_table()

    count_f = counts_ref[...].astype(F32)
    down = lax.broadcasted_iota(jnp.int32, (cols, rows), 0)
    along = lax.broadcasted_iota(jnp.int32, (cols, rows), 1)

    def pick(row, column):
        begin = jnp.sum(
            jnp.where((down == column) & (along < row), count_f, 0.0), keepdims=True
        )
        count = jnp.sum(
            jnp.where((down == column) & (along == row), count_f, 0.0), keepdims=True
        )
        return begin + (column * column_width).astype(F32), count

    for s, (row, column) in enumerate(((i, j),) + across):
        begin, count = pick(row, column)
        rank = lax.broadcasted_iota(jnp.int32, (slots, 1), 0).astype(F32)
        number = jnp.where(rank < count, begin + rank, -1.0)
        if direct:
            lane = lax.broadcasted_iota(jnp.int32, (slots, order), 1)
            pick_table[0, pl.ds(s * slots, slots)] = jnp.where(
                lane.astype(F32) == number, 1.0, 0.0
            ).astype(BF16)
            continue
        lane = lax.broadcasted_iota(jnp.int32, (slots, rows * block_half), 1)
        for h in range(2):
            a = (lane // block_half) * block_rows + lax.rem(lane, block_half) + h * block_half
            pick_table[h, pl.ds(s * slots, slots)] = jnp.where(
                a.astype(F32) == number, 1.0, 0.0
            ).astype(BF16)

    for f in range(FACES):
        face_wait(0, f)
        r_f[f] = out_face[0, f].astype(F32) - in_face[0, f].astype(F32)

    def precondition(turn, use):
        w_box, v_box = weight_box.at[turn], value_box.at[turn]
        w_number, v_number, o_number = (sums + 1 + 3 * turn + n for n in range(3))
        weights = jnp.zeros((slots, cases), F32)
        for f in range(FACES):
            rounded = r_f[f].astype(BF16)
            weights = weights + mm_nt(modes[:, f * face : (f + 1) * face], rounded)
            moved[:, f * face : (f + 1) * face] = (rounded.astype(F32) * scale[f]).astype(BF16)
        if direct:
            w_box[pl.ds(i, 1)] = pack(weights).astype(BF16)[None]
            to_column(w_box, w_number)
        else:
            w_box[pl.ds(me, 1)] = pack(weights).astype(BF16)[None]
            to_all(w_box, w_number)

        total_f = jnp.zeros((cases, face), F32)
        for pair in PAIRS:
            for f in pair:
                if turn == 0:
                    get_dirichlet[f].wait()
            for f in pair:
                out_face[use, f] = mm(moved[...], dirichlet[f]).astype(BF16)
            for f in pair:
                face_start(use, f)
        for f in range(FACES):
            total_f = total_f + (r_f[f] * scale[f]) * out_face[use, f].astype(F32)
        row = row_sum(total_f)

        both = jnp.concatenate([row, row], axis=1)
        if direct:
            if turn > 0:
                share_sum(2 * turn, both)
            else:
                direct_table()
            all_of(w_box, w_number).wait_recv()
            out = mm(weight_table[...], unpack(w_box[...].reshape(rows * half, 2 * cases)).astype(BF16))
            v_box[pl.ds(j, 1)] = pack(out[:order])[None]
            own_box[turn, pl.ds(j, 1)] = pack(out[order:]).astype(BF16)[None]
            to_row(v_box, v_number)
            to_row(own_box.at[turn], o_number)
        else:
            all_of(w_box, w_number).wait_recv()
            out = mm(weight_table[...], w_box[...].reshape(total * half, 2 * cases))
            b = block_rows
            values = (out[:b, :cases] + out[b : 2 * b, cases:]).astype(BF16)
            own = out[2 * b : 3 * b, :cases] + out[3 * b :, cases:]
            v_box[pl.ds(i, 1)] = pack(values.astype(F32)).astype(BF16)[None]
            to_column(v_box, v_number)
            inner = jnp.sum(values.astype(F32) * own, axis=0, keepdims=True)
            row = row + widen(inner) * jnp.where(j == 0, 1.0, 0.0)
            if turn > 0:
                share_sum(2 * turn, jnp.concatenate([row, row], axis=1))

        for f in range(FACES):
            face_wait(use, f)
            local = out_face[use, f].astype(F32) - in_face[use, f].astype(F32)
            z_f[f] = local
            gz_f[f] = -local * have[f]
        if turn == 0:
            for f in range(FACES):
                @pl.when(exists[f])
                def _():
                    modes_copy(f, f).wait_recv()

        all_of(v_box, v_number).wait_recv()
        extra = jnp.zeros((1, 128), F32)
        if direct:
            all_of(own_box.at[turn], o_number).wait_recv()
            values = unpack(jnp.sum(v_box[...], axis=0)).astype(BF16)
            own = jnp.concatenate([unpack(own_box[turn, k]) for k in range(cols)], axis=0)
            extra = widen(jnp.sum(values.astype(F32) * own, axis=0, keepdims=True))
            picked = mm(pick_table[0], values)
        else:
            flat = v_box[...].reshape(rows * block_half, 2 * cases)
            picked = mm(pick_table[0], flat)[:, :cases] + mm(pick_table[1], flat)[:, cases:]
        own_picked = picked[:slots].T.astype(BF16)
        for f in range(FACES):
            z_f[f] = z_f[f] + mm(own_picked, modes[:, f * face : (f + 1) * face])
            gz_f[f] = gz_f[f] + mm_tn(picked[(1 + f) * slots : (2 + f) * slots], near_modes[f])
        return row, extra

    first_energy, extra = precondition(0, 1)
    energy = None
    use = 2
    for turn in range(ITERS):
        if turn == 0:
            for f in range(FACES):
                d_f[f] = z_f[f]
                g_f[f] = gz_f[f]
        else:
            fresh = take_sum(2 * turn)[:, :128] + extra
            beta = as_column(fresh / energy)
            energy = fresh
            for f in range(FACES):
                d_f[f] = z_f[f] + beta * d_f[f]
                g_f[f] = gz_f[f] + beta * g_f[f]
        for f in range(FACES):
            moved[:, f * face : (f + 1) * face] = (
                d_f[f].astype(BF16).astype(F32) - g_f[f].astype(BF16).astype(F32)
            ).astype(BF16)
        total_f = jnp.zeros((cases, face), F32)
        for f in range(FACES):
            image = mm(moved[...], flex[f]).astype(BF16)
            out_face[use, f] = image
            total_f = total_f + (d_f[f] - g_f[f]) * image.astype(F32)
        row = row_sum(total_f)
        for f in PAIRS[0]:
            face_start(use, f)
        share_sum(2 * turn + 1, jnp.concatenate([row, first_energy], axis=1))
        for f in PAIRS[1]:
            face_start(use, f)
        for f in range(FACES):
            face_wait(use, f)
        for f in range(FACES):
            z_f[f] = out_face[use, f].astype(F32) - in_face[use, f].astype(F32)
        both = take_sum(2 * turn + 1)
        if turn == 0:
            energy = both[:, 128:] + extra
        step = as_column(energy / both[:, :128])
        for f in range(FACES):
            residual = r_f[f] - step * z_f[f]
            advance = step * d_f[f]
            if turn > 0:
                advance = x_f[f] + advance
            if turn + 1 < ITERS:
                r_f[f] = residual
                x_f[f] = advance
            else:
                mult_ref[:, f * face : (f + 1) * face] = advance.astype(BF16)
                resid_ref[:, f * face : (f + 1) * face] = residual.astype(BF16)
        use += 1
        if turn + 1 < ITERS:
            _, extra = precondition(turn + 1, use)
            use += 1

    for f in range(FACES):
        @pl.when(exists[f])
        def _():
            modes_copy(f, OPPOSITE[f]).wait_send()
            for use in range(2 * ITERS + 1):
                face_copy(use, f).wait_send()
    for number in range(1, sums):
        all_of(sum_box.at[number], number).wait_send()
    all_of(inverse, sums).wait_send()
    for turn in range(ITERS):
        all_of(weight_box.at[turn], sums + 1 + 3 * turn).wait_send()
        all_of(value_box.at[turn], sums + 2 + 3 * turn).wait_send()
        if direct:
            all_of(own_box.at[turn], sums + 3 + 3 * turn).wait_send()


def settle(mult_in, resid_in, mult_out, resid_out):
    mult_out[...] = mult_in[...]
    resid_out[...] = resid_in[...]


def shards(rows, cols, loads, flexibility, dirichlet, modes, coarse_inverse, mode_counts):
    _, _, cases, width = loads.shape
    slots = modes.shape[2]
    block_rows, column_width = coarse_inverse.shape
    total = rows * cols
    face = width // FACES
    uses = 2 * ITERS + 1
    bulks = 2 * ITERS + 1 + 3 * ITERS
    half, order = slots // 2, cols * column_width
    direct = order * column_width <= 1 << 20
    if direct:
        coarse = [
            pltpu.VMEM((order + column_width, rows * slots), BF16),
            pltpu.VMEM((1, (1 + FACES) * slots, order), BF16),
            pltpu.VMEM((ITERS, rows, half, 2 * cases), BF16),
            pltpu.VMEM((ITERS, cols, order // 2, 2 * cases), F32),
        ]
    else:
        coarse = [
            pltpu.VMEM((4 * block_rows, total * half), BF16),
            pltpu.VMEM((2, (1 + FACES) * slots, rows * block_rows // 2), BF16),
            pltpu.VMEM((ITERS, total, half, 2 * cases), BF16),
            pltpu.VMEM((ITERS, rows, block_rows // 2, 2 * cases), BF16),
        ]
    anywhere = pl.BlockSpec(memory_space=pl.ANY)
    inside = pl.BlockSpec(memory_space=pltpu.VMEM)
    field = pltpu.VMEM((FACES, cases, face), F32)
    dma = pltpu.SemaphoreType.DMA
    mult, resid = pl.pallas_call(
        functools.partial(kernel, rows, cols, direct),
        out_shape=[jax.ShapeDtypeStruct((cases, width), BF16)] * 2,
        in_specs=[anywhere] * 6,
        out_specs=[inside] * 2,
        scratch_shapes=[
            pltpu.VMEM((cases, width), BF16),
            pltpu.VMEM((FACES, width, face), BF16),
            pltpu.VMEM((FACES, width, face), BF16),
            pltpu.VMEM((slots, width), BF16),
            pltpu.VMEM((rows if direct else cols, block_rows, column_width), BF16),
            pltpu.VMEM((cols, rows), jnp.int32),
            pltpu.VMEM((FACES, slots, face), BF16),
            *coarse,
            pltpu.VMEM((ITERS, cols, column_width // 2, 2 * cases), BF16),
            pltpu.VMEM((2 * ITERS, total, 1, 256), F32),
            pltpu.VMEM((uses, FACES, cases, face), BF16),
            pltpu.VMEM((uses, FACES, cases, face), BF16),
            pltpu.VMEM((cases, width), BF16),
            field, field, field, field, field, field,
            dma((12,)),
            dma((uses, FACES)),
            dma((uses, FACES)),
            dma((FACES,)),
            dma((FACES,)),
            dma((bulks,)),
            dma((bulks,)),
        ],
        compiler_params=pltpu.CompilerParams(
            collective_id=0, has_side_effects=True, vmem_limit_bytes=62 * 1024 * 1024
        ),
    )(
        loads.reshape(cases, width),
        flexibility.reshape(width, width),
        dirichlet.reshape(width, width),
        modes.reshape(slots, width),
        coarse_inverse,
        mode_counts,
    )
    mult, resid = pl.pallas_call(
        settle,
        out_shape=[jax.ShapeDtypeStruct((cases, width), BF16)] * 2,
        in_specs=[inside] * 2,
        out_specs=[inside] * 2,
        compiler_params=pltpu.CompilerParams(vmem_limit_bytes=62 * 1024 * 1024),
    )(mult, resid)
    return mult[None, None], resid[None, None]


def solution(mesh):
    return jax.shard_map(
        functools.partial(shards, mesh.shape["wide"], mesh.shape["narrow"]),
        mesh=mesh,
        in_specs=(
            P("wide", "narrow", None, None),
            P("wide", "narrow", None, None),
            P("wide", "narrow", None, None),
            P("wide", "narrow", None, None),
            P("wide", "narrow"),
            P(),
        ),
        out_specs=(P("wide", "narrow", None, None), P("wide", "narrow", None, None)),
        check_vma=False,
    )
```
